32 devices in a mesh: grp: 2 (over y), loc: 2 (over x), dp: 8 (over z, core).
Axes of the slice: x: 2, y: 2, z: 4, core: 2. Of those that a mesh axis runs over, the one named last changes fastest.
Arguments:
- out_grad: bfloat16 [8, 256, 7168], P('dp', ('grp', 'loc')), may hold values from -6 to 6
- slot_token: int32 [8, 4, 2, 5], P('dp', ('grp', 'loc')), may hold values from 0 to 63, as said below
- slot_count: int32 [8, 4, 2], P('dp', ('grp', 'loc')), may hold values from 1 to 5, as said below
- slot_weight: bfloat16 [8, 4, 2, 5], P('dp', ('grp', 'loc')), may hold values from 0.049804688 to 0.59765625
- up_weight: bfloat16 [2, 7168, 512], P('grp', None, 'loc'), may hold values from -0.0625 to 0.0625
- down_weight: bfloat16 [2, 512, 7168], P('grp', 'loc'), may hold values from -0.25 to 0.25
- hidden_saved: bfloat16 [8, 2, 20, 512], P('dp', 'grp', None, 'loc'), may hold values from -6 to 6
- gate_saved: bfloat16 [8, 2, 20, 512], P('dp', 'grp', None, 'loc'), may hold values from -6 to 6
Outputs:
- input_grad: bfloat16 [8, 256, 7168], P('dp', ('grp', 'loc'))
- down_grad: float32 [2, 512, 7168], P('grp', ('loc', 'dp'))
The draws below stay inside these ranges and needn't reach their ends.
Inputs may be any that keep to these rules, and one draw needn't show every extreme that they name: `slot_token`: within one replica, source device and expert the first slot_count slots name different tokens; later entries are arbitrary tokens of the range. `slot_count`: every source device fills all 5 slots of some expert, and in every replica some expert has all 5 slots filled from every source device.
All inputs are finite; a program needn't handle non-finite values.
Results may differ from the reference program's by a relative error of at most 0.012.
Values may be sent and summed in bfloat16 or wider, within the bound.
No kernel may reach another device: no remote copies, remote signals or barrier semaphores. Data moves between devices by JAX's collectives and lax.ppermute only.
A program may use at most 64 MiB of HBM per device.

```python
import jax
import jax.numpy as jnp
from jax import lax

D = 7168
H_DEV = 256
CAP = 5
TOK_DEV = 64
FF = 512
TOK_REP = 256
SLOTS = 20
N_GRP = 2
N_LOC = 2
N_DP = 8


def draw_slot_token(key, part):
    key = jax.random.fold_in(key, 11)
    scores = jax.random.randint(key, (N_DP, N_GRP * N_LOC, N_GRP, TOK_DEV), 0, 1 << 20) * TOK_DEV
    scores = scores + jnp.arange(TOK_DEV, dtype=jnp.int32)
    ordering = jnp.argsort(scores, axis=-1, stable=True)
    return ordering[..., :CAP].astype(jnp.int32)


def draw_slot_count(key, part):
    key = jax.random.fold_in(key, 23)
    key_base, key_source, key_replica = jax.random.split(key, 3)
    base_count = jax.random.randint(key_base, (N_DP, N_GRP * N_LOC, N_GRP), 1, CAP + 1)
    full_source = jax.random.randint(key_source, (N_DP, N_GRP * N_LOC, 1), 0, N_GRP)
    full_replica = jax.random.randint(key_replica, (N_DP, 1, 1), 0, N_GRP)
    experts = jnp.arange(N_GRP, dtype=jnp.int32)[None, None, :]
    filled = (experts == full_source) | (experts == full_replica)
    return jnp.where(filled, CAP, base_count).astype(jnp.int32)


def block_levels(own_key, dims, cuts, low, largest):
    gain, own = 1.0, jax.random.fold_in(own_key, 6)
    for dim, shards_of in cuts:
        steps = jnp.exp(jax.random.uniform(jax.random.fold_in(own, dim), (shards_of,), jnp.float32, low / len(cuts), largest / len(cuts)))
        gain = gain * jnp.repeat(steps, dims[dim] // shards_of).reshape([-1 if axis == dim else 1 for axis in range(len(dims))])
    return gain


def gaussian(stream_key, dims, width, most, cuts=(), kind=jnp.bfloat16):
    gain = block_levels(stream_key, dims, cuts, -0.22, 0.18) if cuts else 1.0
    entries = jax.random.normal(stream_key, dims, jnp.float32) * width * gain
    return jnp.minimum(jnp.maximum(entries, -most), most).astype(kind)


def setup_inputs(seed: int = 0) -> dict:
    keys = jax.random.split(jax.random.key(seed), 9)
    return {
        "out_grad": gaussian(keys[0], (N_DP, TOK_REP, D), 1.0, 6.0, ((0, 8), (1, 4))),
        "slot_token": draw_slot_token(jax.random.fold_in(keys[8], 71), 0),
        "slot_count": draw_slot_count(jax.random.fold_in(keys[8], 71), 0),
        "slot_weight": jnp.clip(0.049804688 + 0.54785156 * jax.random.uniform(keys[3], (N_DP, N_GRP * N_LOC, N_GRP, CAP), jnp.float32) ** block_levels(keys[3], (N_DP, N_GRP * N_LOC, N_GRP, CAP), ((0, 8), (1, 4)), -0.2, 0.2), 0.049804688, 0.59765625).astype(jnp.bfloat16),
        "up_weight": gaussian(keys[4], (N_GRP, D, FF), D ** -0.5, 0.0625, ((0, 2), (2, 2))),
        "down_weight": gaussian(keys[5], (N_GRP, FF, D), FF ** -0.5, 0.25, ((0, 2), (1, 2))),
        "hidden_saved": gaussian(keys[6], (N_DP, N_GRP, SLOTS, FF), 1.0, 6.0, ((0, 8), (1, 2), (3, 2))),
        "gate_saved": gaussian(keys[7], (N_DP, N_GRP, SLOTS, FF), 1.0, 6.0, ((0, 8), (1, 2), (3, 2))),
    }


def reference(out_grad, slot_token, slot_count, slot_weight, up_weight, down_weight, hidden_saved, gate_saved):
    sources = N_GRP * N_LOC
    live_all = jnp.arange(CAP, dtype=jnp.int32)[None, None, None, :] < slot_count[..., None]
    offsets = (jnp.arange(sources, dtype=jnp.int32) * TOK_DEV)[None, :, None, None]
    index_all = (slot_token + offsets).astype(jnp.int32)

    def replica(running, inputs):
        grad_rows, slot_index, live_mask, weights, hidden, gate_act = inputs
        token_sum = jnp.zeros((TOK_REP, D), jnp.float32)
        for expert in range(N_GRP):
            flat_index = slot_index[:, expert, :].reshape(-1).astype(jnp.int32)
            flat_live = live_mask[:, expert, :].reshape(-1)
            slot_rows = jnp.where(flat_live[:, None], grad_rows[flat_index], jnp.zeros((), jnp.bfloat16))
            slot_scale = weights[:, expert, :].reshape(-1).astype(jnp.float32)[:, None]
            grad_act = jnp.dot(slot_rows, down_weight[expert].T, preferred_element_type=jnp.float32)
            grad_up = (slot_scale * grad_act * gate_act[expert].astype(jnp.float32)).astype(jnp.bfloat16)
            partial_value = jnp.einsum("snh,dnh->nsd",
                                 grad_up.reshape(SLOTS, N_LOC, H_DEV).astype(jnp.float32),
                                 up_weight[expert].reshape(D, N_LOC, H_DEV).astype(jnp.float32)).astype(jnp.bfloat16)
            contrib = jnp.sum(partial_value.astype(jnp.float32), axis=0).astype(jnp.bfloat16)
            token_sum = token_sum.at[flat_index].add(contrib.astype(jnp.float32))
            weighted = (slot_scale * hidden[expert].astype(jnp.float32)).astype(jnp.bfloat16)
            weight_term = jnp.dot(weighted.T, slot_rows, preferred_element_type=jnp.float32).astype(jnp.bfloat16)
            running = running.at[expert].add(weight_term.astype(jnp.float32))
        return running, token_sum.astype(jnp.bfloat16)

    start_sum = jnp.zeros((N_GRP, FF, D), jnp.float32)
    summed_grad, input_grad = lax.scan(replica, start_sum,
                                       (out_grad, index_all, live_all, slot_weight, hidden_saved, gate_saved))
    down_grad = summed_grad / N_DP
    return input_grad, down_grad
```

```python
import functools

import jax
import jax.numpy as jnp
from jax import lax
from jax.experimental import pallas as pl
from jax.experimental.pallas import tpu as pltpu
from jax.sharding import PartitionSpec as P

AXES = ("grp", "loc", "dp")
PIECES = 8
F32 = jnp.float32
BF16 = jnp.bfloat16


def local_collectives(
    out_grad, slot_token, slot_count, slot_weight, up_weight, down_weight, hidden_saved, gate_saved
):
    group_count = lax.axis_size("grp")
    local_count = lax.axis_size("loc")
    replicas = lax.axis_size("dp")
    grad_rows = out_grad[0]
    tok_dev = grad_rows.shape[0]
    model_dim = grad_rows.shape[1]
    tokens = slot_token[0, 0]
    capacity = tokens.shape[1]
    live_mask = jnp.arange(capacity, dtype=jnp.int32)[None, :] < slot_count[0, 0][:, None]
    picked = jnp.take(grad_rows, tokens.reshape(-1), axis=0).reshape(
        group_count, capacity, model_dim
    )
    outgoing = jnp.where(live_mask[:, :, None], picked, jnp.zeros((), jnp.bfloat16))
    weights = slot_weight[0, 0]
    arrived, arrived_weights = (
        lax.all_to_all(outgoing, "grp", split_axis=0, concat_axis=0, tiled=True),
        lax.all_to_all(weights, "grp", split_axis=0, concat_axis=0, tiled=True),
    )
    rows_all, weights_all = (
        lax.all_gather(arrived[:, None], "loc", axis=1, tiled=True),
        lax.all_gather(arrived_weights[:, None], "loc", axis=1, tiled=True),
    )
    slot_total = group_count * local_count * capacity
    slot_rows = rows_all.reshape(slot_total, model_dim)
    slot_scale = weights_all.reshape(slot_total).astype(jnp.float32)[:, None]
    hidden = hidden_saved[0, 0]
    gate_act = gate_saved[0, 0]
    w_down = down_weight[0]
    w_up = up_weight[0]
    grad_act = lax.dot_general(
        slot_rows, w_down, (((1,), (1,)), ((), ())), preferred_element_type=jnp.float32
    )
    grad_up = (slot_scale * grad_act * gate_act.astype(jnp.float32)).astype(jnp.bfloat16)
    partial_value = lax.dot_general(
        grad_up, w_up, (((1,), (1,)), ((), ())), preferred_element_type=jnp.float32
    )
    partial_value = partial_value.astype(jnp.bfloat16)
    weighted = (slot_scale * hidden.astype(jnp.float32)).astype(jnp.bfloat16)
    product = lax.dot_general(
        weighted, slot_rows, (((0,), (0,)), ((), ())), preferred_element_type=jnp.float32
    )
    rounded = lax.optimization_barrier(product.astype(jnp.bfloat16))
    summed = lax.psum_scatter(
        rounded.astype(jnp.float32).astype(jnp.bfloat16), "dp", scatter_dimension=0, tiled=True
    ).astype(jnp.float32)
    down_grad = (summed / replicas)[None]
    term_rows = lax.optimization_barrier(partial_value).astype(jnp.float32)
    term_rows = term_rows.reshape(group_count, local_count, capacity, model_dim)
    summed_rows = lax.psum_scatter(
        term_rows.astype(jnp.bfloat16), "loc", scatter_dimension=1, tiled=True
    )
    returned = lax.all_to_all(summed_rows, "grp", split_axis=0, concat_axis=0, tiled=True)
    contribs = returned.reshape(group_count * capacity, model_dim)
    matches = jnp.arange(tok_dev, dtype=jnp.int32)[:, None] == tokens.reshape(-1)[None, :]
    onehot = (matches & live_mask.reshape(-1)[None, :]).astype(jnp.bfloat16)
    input_grad = jnp.dot(onehot, contribs, preferred_element_type=jnp.float32).astype(jnp.bfloat16)[
        None
    ]
    return (input_grad, down_grad)


def iota(shape, dim):
    return lax.broadcasted_iota(jnp.int32, shape, dim)


def quotient(value, cap, most):
    shift = 16
    factor = (1 << shift) // cap + 1
    assert all((v * factor) >> shift == v // cap for v in range(most))
    return lax.shift_right_logical(value * factor, shift)


def dot(a, b):
    return jnp.dot(a, b, preferred_element_type=F32)


def dot_nt(a, b):
    return lax.dot_general(a, b, (((1,), (1,)), ((), ())), preferred_element_type=F32)


def hot(condition):
    return jnp.where(condition, 1.0, 0.0).astype(BF16)


def place():
    group, loc, dp = (lax.axis_index(axis) for axis in AXES)
    z = dp // 2
    return group, loc, z % 2, z // 2, dp % 2


def select_kernel(tok, cnt, weight, rows, hidden, near, far):
    cap = tok.shape[3]
    group, _, _, _, _ = place()
    tokens, model = rows.shape[1], rows.shape[2]
    piece_cols = model // PIECES
    count = PIECES * cap
    scale = weight[0, 0].astype(F32)
    row, token = iota((count, tokens), 0), iota((count, tokens), 1)
    piece = quotient(row, cap, count)
    slot = row - cap * piece
    for other, out in ((0, near), (1, far)):
        expert = jnp.where(group == other, 0, 1)
        live = cnt[0, 0, expert]
        value = jnp.zeros((count, tokens), F32)
        for s in range(cap):
            name = jnp.where(s < live, tok[0, 0, expert, s], -1)
            factor = jnp.where(
                expert == 0, scale[0:1, s : s + 1], scale[1:2, s : s + 1]
            )
            value = jnp.where((slot == s) & (token == name), factor, value)
        total = jnp.zeros((count, piece_cols), F32)
        for j in range(PIECES):
            chosen = jnp.where(piece == j, value, 0.0).astype(BF16)
            total += dot(chosen, rows[0, :, j * piece_cols : (j + 1) * piece_cols])
        out[:, :piece_cols] = total.astype(BF16)
    half = hidden.shape[3] // 2
    slots = hidden.shape[2]
    r, c = iota((count, slots), 0), iota((count, slots), 1)
    folded = dot(hot(r == c), hidden[0, 0, :, :half]) + dot(
        hot(r == c + slots), hidden[0, 0, :, half:]
    )
    near[:, piece_cols:] = folded.astype(BF16)


def spread_kernel(own, from_x, from_y, from_xy, keep, to_1, to_2, to_3):
    count, piece_cols = from_y.shape
    cap = count // PIECES
    slots = 4 * cap
    group, loc, zb, pair, _ = place()
    source = 2 * group + loc
    m, n = iota((2 * count, count), 0), iota((2 * count, count), 1)
    mq, nq = quotient(m, cap, 2 * count), quotient(n, cap, count)
    m_slot, n_slot = m - cap * mq, n - cap * nq
    m_flip, m_source, m_part = mq >> 3, (mq >> 1) & 3, mq & 1
    wanted = 4 * loc + 2 * (zb ^ m_flip) + m_part
    rows_ok = (m_slot == n_slot) & (nq == wanted)
    total = jnp.zeros((2 * count, piece_cols), F32)
    for k, ref in enumerate((own, from_x, from_y, from_xy)):
        total += dot(hot(rows_ok & (m_source == (source ^ k))), ref[:, :piece_cols])
    m_loc, m_row = (mq >> 2) & 1, m - slots * (mq >> 2)
    n_half, n_row = nq >> 2, n - slots * (nq >> 2)
    hidden_ok = (m_row == n_row) & (n_half == (pair ^ m_flip))
    hidden = dot(hot(hidden_ok & (m_loc == loc)), own[:, piece_cols:]) + dot(
        hot(hidden_ok & (m_loc != loc)), from_x[:, piece_cols:]
    )
    total, hidden = total.astype(BF16), hidden.astype(BF16)
    for ref, flip_zb, flip_pair in ((keep, 0, 0), (to_1, 1, 0), (to_2, 0, 1), (to_3, 1, 1)):
        ref[:, :piece_cols] = total[flip_zb * count : (flip_zb + 1) * count]
        ref[:, piece_cols:] = hidden[flip_pair * count : (flip_pair + 1) * count]


def expert_kernel(
    own, from_x, from_y, from_xy, down, gate, up, ret_own, ret_x, ret_y, ret_xy, stack
):
    count, piece_cols = from_y.shape
    cap = count // PIECES
    pad = stack.shape[0] // PIECES
    slots = gate.shape[2]
    group, loc, _, _, _ = place()
    source = 2 * group + loc
    m, n = iota((PIECES * pad, count), 0), iota((PIECES * pad, count), 1)
    nq = quotient(n, cap, count)
    n_slot = n - cap * nq
    m_piece, m_slot = m // pad, m % pad
    total = jnp.zeros((PIECES * pad, piece_cols), F32)
    for k, ref in enumerate((own, from_x, from_y, from_xy)):
        match = (m_piece == nq) & (m_slot == (source ^ k) * cap + n_slot)
        total += dot(hot(match), ref[:, :piece_cols])
    slot_rows = total.astype(BF16)
    grad_act = jnp.zeros((pad, down.shape[1]), F32)
    for j in range(PIECES):
        grad_act += dot_nt(
            slot_rows[j * pad : (j + 1) * pad], down[0, :, j * piece_cols : (j + 1) * piece_cols]
        )
    gate_pad = dot(hot(iota((pad, slots), 0) == iota((pad, slots), 1)), gate[0, 0])
    grad_up = (grad_act * gate_pad).astype(BF16)
    for j in range(PIECES):
        part = dot_nt(grad_up, up[0, j * piece_cols : (j + 1) * piece_cols, :])
        stack[j * pad : (j + 1) * pad, :] = part.astype(BF16)
    n, m = iota((count, PIECES * pad), 0), iota((count, PIECES * pad), 1)
    nq = quotient(n, cap, count)
    n_slot = n - cap * nq
    m_piece, m_slot = m // pad, m % pad
    for k, ref in enumerate((ret_own, ret_x, ret_y, ret_xy)):
        match = (m_piece == nq) & (m_slot == (source ^ k) * cap + n_slot)
        ref[...] = dot(hot(match), stack[...]).astype(BF16)


def combine_kernel(tok, cnt, own, from_x, from_y, from_xy, out):
    count, piece_cols = own.shape
    cap = tok.shape[3]
    tokens = out.shape[1]
    group, _, _, _, _ = place()
    m, n = iota((tokens, count), 0), iota((tokens, count), 1)
    nq = quotient(n, cap, count)
    n_slot = n - cap * nq
    pairs = []
    for other, (a, b) in enumerate(((own, from_x), (from_y, from_xy))):
        contrib = (a[...].astype(F32) + b[...].astype(F32)).astype(BF16)
        expert = jnp.where(group == other, 0, 1)
        live = cnt[0, 0, expert]
        match = jnp.zeros((tokens, count), F32)
        for s in range(cap):
            name = jnp.where(s < live, tok[0, 0, expert, s], -1)
            match = jnp.where((n_slot == s) & (m == name), 1.0, match)
        pairs.append((match, contrib))
    for j in range(PIECES):
        total = jnp.zeros((tokens, piece_cols), F32)
        for match, contrib in pairs:
            total += dot(jnp.where(nq == j, match, 0.0).astype(BF16), contrib)
        out[0, :, j * piece_cols : (j + 1) * piece_cols] = total.astype(BF16)


def product_kernel(scale, own, from_1, from_2, from_3, keep, send):
    count = own.shape[0]
    cap = count // PIECES
    slots = 4 * cap
    half = own.shape[1] - keep.shape[1] // 2
    piece_cols = own.shape[1] - half
    _, _, _, _, core = place()
    refs = (own, from_1, from_2, from_3)
    rows = jnp.concatenate([ref[:, :piece_cols].astype(F32) for ref in refs], 0).astype(BF16)
    m, n = iota((4 * count, count), 0), iota((4 * count, count), 1)
    mq = quotient(m, cap, 4 * count)
    m_slot = m - cap * mq
    m_part, m_loc, m_source, m_has = mq >> 4, (mq >> 3) & 1, (mq >> 1) & 3, mq & 1
    nq = quotient(n, cap, count)
    n_loc, n_row = nq >> 2, n - slots * (nq >> 2)
    ok = (m_has == m_part) & (m_loc == n_loc) & (m_source * cap + m_slot == n_row)
    place_rows = jnp.where(ok, scale, 0.0).astype(BF16)
    spread = [dot(place_rows, ref[:, piece_cols:]) for ref in refs]
    rows_dev = half // 4
    for part in range(2):
        for loc in range(2):
            at = (2 * part + loc) * count
            hidden = jnp.concatenate([value[at : at + count] for value in spread], 0)
            product = dot(hidden.T.astype(BF16), rows)
            for zb in range(2):
                base = zb * 2 * rows_dev
                first = product[base : base + rows_dev]
                second = product[base + rows_dev : base + 2 * rows_dev]
                block = slice((2 * loc + zb) * rows_dev, (2 * loc + zb + 1) * rows_dev)
                cols = slice(part * piece_cols, (part + 1) * piece_cols)
                keep[block, cols] = jnp.where(core == 0, first, second).astype(BF16)
                send[block, cols] = jnp.where(core == 0, second, first).astype(BF16)


def add_kernel(mine, other, own, to_x, to_z, to_xz):
    rows_dev = own.shape[0]
    _, loc, zb, _, _ = place()
    for k, out in enumerate((own, to_z, to_x, to_xz)):
        at = pl.ds(pl.multiple_of(((2 * loc + zb) ^ k) * rows_dev, rows_dev), rows_dev)
        out[...] = (mine[at, :].astype(F32) + other[at, :].astype(F32)).astype(BF16)


def join_kernel(own, from_x, from_z, from_xz, out):
    cols = own.shape[1]
    _, loc, zb, _, _ = place()
    for k, ref in enumerate((own, from_z, from_x, from_xz)):
        at = pl.ds(pl.multiple_of(((2 * loc + zb) ^ k) * cols, cols), cols)
        out[0, :, at] = ref[...].astype(F32)


VM = pl.BlockSpec(memory_space=pltpu.VMEM)
SM = pl.BlockSpec(memory_space=pltpu.SMEM)


def call(kernel, outs, args, specs=None, scratch=(), flops=0, nbytes=0):
    out_shape = tuple(jax.ShapeDtypeStruct(shape, dtype) for shape, dtype in outs)
    result = pl.pallas_call(
        kernel,
        out_shape=out_shape,
        in_specs=specs or [VM] * len(args),
        out_specs=tuple([VM] * len(outs)),
        scratch_shapes=list(scratch),
        compiler_params=pltpu.CompilerParams(vmem_limit_bytes=40 * 1024 * 1024),
        cost_estimate=pl.CostEstimate(flops=flops, bytes_accessed=nbytes, transcendentals=0),
    )(*args)
    return result


def swap(value, group_flip=0, loc_flip=0, dp_flip=0):
    sizes = [lax.axis_size(axis) for axis in AXES]
    pairs = []
    for g in range(sizes[0]):
        for l in range(sizes[1]):
            for d in range(sizes[2]):
                here = (g * sizes[1] + l) * sizes[2] + d
                there = ((g ^ group_flip) * sizes[1] + (l ^ loc_flip)) * sizes[2] + (d ^ dp_flip)
                pairs.append((here, there))
    return lax.ppermute(value, AXES, pairs)


def local_messages(
    out_grad, slot_token, slot_count, slot_weight, up_weight, down_weight, hidden_saved, gate_saved
):
    model = out_grad.shape[2]
    tokens = out_grad.shape[1]
    cap = slot_token.shape[3]
    hidden_dev = hidden_saved.shape[3]
    replicas = lax.axis_size("dp")
    piece_cols, half, count = model // PIECES, hidden_dev // 2, PIECES * cap
    rows_dev = hidden_dev // replicas
    near, far = call(
        select_kernel,
        [((count, piece_cols + half), BF16), ((count, piece_cols), BF16)],
        (slot_token, slot_count, slot_weight, out_grad, hidden_saved),
        [SM, SM, VM, VM, VM],
        nbytes=tokens * model * 2,
    )
    from_x = swap(near, loc_flip=1)
    from_y = swap(far, group_flip=1)
    from_xy = swap(far, group_flip=1, loc_flip=1)
    arrived = (near, from_x, from_y, from_xy)
    message = ((count, piece_cols + half), BF16)
    mine, to_1, to_2, to_3 = call(spread_kernel, [message] * 4, arrived, nbytes=count * model)
    from_1 = swap(to_1, dp_flip=2)
    from_2 = swap(to_2, dp_flip=4)
    from_3 = swap(to_3, dp_flip=6)
    pad = -(-4 * cap // 16) * 16
    ret_own, ret_x, ret_y, ret_xy = call(
        expert_kernel,
        [((count, piece_cols), BF16)] * 4,
        arrived + (down_weight, gate_saved, up_weight),
        scratch=[pltpu.VMEM((PIECES * pad, piece_cols), BF16)],
        flops=4 * pad * model * hidden_dev,
        nbytes=4 * model * hidden_dev,
    )
    back_x = swap(ret_x, loc_flip=1)
    back_y = swap(ret_y, group_flip=1)
    back_xy = swap(ret_xy, group_flip=1, loc_flip=1)
    (input_grad,) = call(
        combine_kernel,
        [((1, tokens, model), BF16)],
        (slot_token, slot_count, ret_own, back_x, back_y, back_xy),
        [SM, SM, VM, VM, VM, VM],
        nbytes=2 * tokens * model,
    )
    block = ((4 * rows_dev, 2 * piece_cols), BF16)
    keep, send = call(
        functools.partial(product_kernel, 1.0 / replicas),
        [block] * 2,
        (mine, from_1, from_2, from_3),
        nbytes=16 * rows_dev * piece_cols,
    )
    other = swap(send, dp_flip=1)
    block = ((rows_dev, 2 * piece_cols), BF16)
    own, to_x, to_z, to_xz = call(add_kernel, [block] * 4, (keep, other), nbytes=1 << 20)
    got_x = swap(to_x, loc_flip=1)
    got_z = swap(to_z, dp_flip=2)
    got_xz = swap(to_xz, loc_flip=1, dp_flip=2)
    (down_grad,) = call(
        join_kernel, [((1, rows_dev, model), F32)], (own, got_x, got_z, got_xz), nbytes=1 << 20
    )
    return (input_grad, down_grad)


def local(*args):
    sizes = tuple(lax.axis_size(axis) for axis in AXES)
    model, cap, hidden_dev = args[0].shape[2], args[1].shape[3], args[6].shape[3]
    fits = sizes == (2, 2, 8) and model % (PIECES * 128) == 0
    fits = fits and hidden_dev % 256 == 0 and args[0].shape[1] % 16 == 0 and 4 * cap <= 32
    return (local_messages if fits else local_collectives)(*args)


def solution(mesh):
    return jax.shard_map(
        local,
        mesh=mesh,
        in_specs=(
            P("dp", ("grp", "loc"), None),
            P("dp", ("grp", "loc"), None, None),
            P("dp", ("grp", "loc"), None),
            P("dp", ("grp", "loc"), None, None),
            P("grp", None, "loc"),
            P("grp", "loc", None),
            P("dp", "grp", None, "loc"),
            P("dp", "grp", None, "loc"),
        ),
        out_specs=(P("dp", ("grp", "loc"), None), P("grp", ("loc", "dp"), None)),
        check_vma=False,
    )
```

```python
import functools

import jax
import jax.numpy as jnp
from jax import lax
from jax.experimental import pallas as pl
from jax.experimental.pallas import tpu as pltpu
from jax.sharding import PartitionSpec as P

AXES = ("grp", "loc", "dp")
PIECES = 8
F32 = jnp.float32
BF16 = jnp.bfloat16


def local_collectives(
    out_grad, slot_token, slot_count, slot_weight, up_weight, down_weight, hidden_saved, gate_saved
):
    group_count = lax.axis_size("grp")
    local_count = lax.axis_size("loc")
    replicas = lax.axis_size("dp")
    grad_rows = out_grad[0]
    tok_dev = grad_rows.shape[0]
    model_dim = grad_rows.shape[1]
    tokens = slot_token[0, 0]
    capacity = tokens.shape[1]
    live_mask = jnp.arange(capacity, dtype=jnp.int32)[None, :] < slot_count[0, 0][:, None]
    picked = jnp.take(grad_rows, tokens.reshape(-1), axis=0).reshape(
        group_count, capacity, model_dim
    )
    outgoing = jnp.where(live_mask[:, :, None], picked, jnp.zeros((), jnp.bfloat16))
    weights = slot_weight[0, 0]
    arrived, arrived_weights = (
        lax.all_to_all(outgoing, "grp", split_axis=0, concat_axis=0, tiled=True),
        lax.all_to_all(weights, "grp", split_axis=0, concat_axis=0, tiled=True),
    )
    rows_all, weights_all = (
        lax.all_gather(arrived[:, None], "loc", axis=1, tiled=True),
        lax.all_gather(arrived_weights[:, None], "loc", axis=1, tiled=True),
    )
    slot_total = group_count * local_count * capacity
    slot_rows = rows_all.reshape(slot_total, model_dim)
    slot_scale = weights_all.reshape(slot_total).astype(jnp.float32)[:, None]
    hidden = hidden_saved[0, 0]
    gate_act = gate_saved[0, 0]
    w_down = down_weight[0]
    w_up = up_weight[0]
    grad_act = lax.dot_general(
        slot_rows, w_down, (((1,), (1,)), ((), ())), preferred_element_type=jnp.float32
    )
    grad_up = (slot_scale * grad_act * gate_act.astype(jnp.float32)).astype(jnp.bfloat16)
    partial_value = lax.dot_general(
        grad_up, w_up, (((1,), (1,)), ((), ())), preferred_element_type=jnp.float32
    )
    partial_value = partial_value.astype(jnp.bfloat16)
    weighted = (slot_scale * hidden.astype(jnp.float32)).astype(jnp.bfloat16)
    product = lax.dot_general(
        weighted, slot_rows, (((0,), (0,)), ((), ())), preferred_element_type=jnp.float32
    )
    rounded = lax.optimization_barrier(product.astype(jnp.bfloat16))
    summed = lax.psum_scatter(
        rounded.astype(jnp.float32).astype(jnp.bfloat16), "dp", scatter_dimension=0, tiled=True
    ).astype(jnp.float32)
    down_grad = (summed / replicas)[None]
    term_rows = lax.optimization_barrier(partial_value).astype(jnp.float32)
    term_rows = term_rows.reshape(group_count, local_count, capacity, model_dim)
    summed_rows = lax.psum_scatter(
        term_rows.astype(jnp.bfloat16), "loc", scatter_dimension=1, tiled=True
    )
    returned = lax.all_to_all(summed_rows, "grp", split_axis=0, concat_axis=0, tiled=True)
    contribs = returned.reshape(group_count * capacity, model_dim)
    matches = jnp.arange(tok_dev, dtype=jnp.int32)[:, None] == tokens.reshape(-1)[None, :]
    onehot = (matches & live_mask.reshape(-1)[None, :]).astype(jnp.bfloat16)
    input_grad = jnp.dot(onehot, contribs, preferred_element_type=jnp.float32).astype(jnp.bfloat16)[
        None
    ]
    return (input_grad, down_grad)


def iota(shape, dim):
    return lax.broadcasted_iota(jnp.int32, shape, dim)


def quotient(value, cap, most):
    shift = 16
    factor = (1 << shift) // cap + 1
    assert all((v * factor) >> shift == v // cap for v in range(most))
    return lax.shift_right_logical(value * factor, shift)


def dot(a, b):
    return jnp.dot(a, b, preferred_element_type=F32)


def dot_nt(a, b):
    return lax.dot_general(a, b, (((1,), (1,)), ((), ())), preferred_element_type=F32)


def hot(condition):
    return jnp.where(condition, 1.0, 0.0).astype(BF16)


def place():
    group, loc, dp = (lax.axis_index(axis) for axis in AXES)
    z = dp // 2
    return group, loc, z % 2, z // 2, dp % 2


def select_kernel(
    tok_hbm, cnt_hbm, weight_hbm, rows_hbm, hidden_hbm, near, far, names, tok, cnt, weight, rows,
    hidden, sems
):
    pairs = (
        (tok_hbm, tok), (cnt_hbm, cnt), (weight_hbm, weight), (rows_hbm, rows), (hidden_hbm, hidden)
    )
    copies = [pltpu.make_async_copy(a, b, sems.at[i]) for i, (a, b) in enumerate(pairs)]
    for copy in copies:
        copy.start()
    cap = tok.shape[3]
    group, _, _, _, _ = place()
    tokens, model = rows.shape[1], rows.shape[2]
    piece_cols = model // PIECES
    count = PIECES * cap
    row, token = iota((count, tokens), 0), iota((count, tokens), 1)
    piece = quotient(row, cap, count)
    slot = row - cap * piece
    line, lane = iota(names.shape, 0), iota(names.shape, 1)
    lane_slot = lane - cap * quotient(lane, cap, names.shape[1])
    for copy in copies[:3]:
        copy.wait()
    scale = weight[0, 0].astype(F32)
    named = jnp.full(names.shape, -1, jnp.int32)
    values = []
    for other in range(2):
        expert = jnp.where(group == other, 0, 1)
        live = cnt[0, 0, expert]
        value = jnp.zeros((count, tokens), F32)
        for s in range(cap):
            name = jnp.where(s < live, tok[0, 0, expert, s], -1)
            factor = jnp.where(
                expert == 0, scale[0:1, s : s + 1], scale[1:2, s : s + 1]
            )
            value = jnp.where((slot == s) & (token == name), factor, value)
            named = jnp.where((line == other) & (lane_slot == s), name, named)
        values.append(value)
    names[...] = named
    for copy in copies[3:]:
        copy.wait()
    for value, out in zip(values, (near, far)):
        total = jnp.zeros((count, piece_cols), F32)
        for j in range(PIECES):
            chosen = jnp.where(piece == j, value, 0.0).astype(BF16)
            total += dot(chosen, rows[0, :, j * piece_cols : (j + 1) * piece_cols])
        out[:, :piece_cols] = total.astype(BF16)
    half = hidden.shape[3] // 2
    slots = hidden.shape[2]
    r, c = iota((count, slots), 0), iota((count, slots), 1)
    folded = dot(hot(r == c), hidden[0, 0, :, :half]) + dot(
        hot(r == c + slots), hidden[0, 0, :, half:]
    )
    near[:, piece_cols:] = folded.astype(BF16)


def load_kernel(down_hbm, up_hbm, gate_hbm, after, down, up, gate, sems):
    pairs = ((down_hbm, down), (up_hbm, up), (gate_hbm, gate))
    copies = [pltpu.make_async_copy(a, b, sems.at[i]) for i, (a, b) in enumerate(pairs)]
    for copy in copies:
        copy.start()
    for copy in copies:
        copy.wait()


def spread_kernel(own, from_x, from_y, from_xy, after, keep, to_1, to_2, to_3):
    count, piece_cols = from_y.shape
    cap = count // PIECES
    slots = 4 * cap
    group, loc, zb, pair, _ = place()
    source = 2 * group + loc
    m, n = iota((2 * count, count), 0), iota((2 * count, count), 1)
    mq, nq = quotient(m, cap, 2 * count), quotient(n, cap, count)
    m_slot, n_slot = m - cap * mq, n - cap * nq
    m_flip, m_source, m_part = mq >> 3, (mq >> 1) & 3, mq & 1
    wanted = 4 * loc + 2 * (zb ^ m_flip) + m_part
    rows_ok = (m_slot == n_slot) & (nq == wanted)
    total = jnp.zeros((2 * count, piece_cols), F32)
    for k, ref in enumerate((own, from_x, from_y, from_xy)):
        total += dot(hot(rows_ok & (m_source == (source ^ k))), ref[:, :piece_cols])
    m_loc, m_row = (mq >> 2) & 1, m - slots * (mq >> 2)
    n_half, n_row = nq >> 2, n - slots * (nq >> 2)
    hidden_ok = (m_row == n_row) & (n_half == (pair ^ m_flip))
    hidden = dot(hot(hidden_ok & (m_loc == loc)), own[:, piece_cols:]) + dot(
        hot(hidden_ok & (m_loc != loc)), from_x[:, piece_cols:]
    )
    total, hidden = total.astype(BF16), hidden.astype(BF16)
    for ref, flip_zb, flip_pair in ((keep, 0, 0), (to_1, 1, 0), (to_2, 0, 1), (to_3, 1, 1)):
        ref[:, :piece_cols] = total[flip_zb * count : (flip_zb + 1) * count]
        ref[:, piece_cols:] = hidden[flip_pair * count : (flip_pair + 1) * count]


def expert_kernel(
    own, from_x, from_y, from_xy, down, gate, up, ret_own, ret_x, ret_y, ret_xy, stack
):
    count, piece_cols = from_y.shape
    cap = count // PIECES
    pad = stack.shape[0] // PIECES
    slots = gate.shape[2]
    group, loc, _, _, _ = place()
    source = 2 * group + loc
    m, n = iota((PIECES * pad, count), 0), iota((PIECES * pad, count), 1)
    nq = quotient(n, cap, count)
    n_slot = n - cap * nq
    m_piece, m_slot = m // pad, m % pad
    total = jnp.zeros((PIECES * pad, piece_cols), F32)
    for k, ref in enumerate((own, from_x, from_y, from_xy)):
        match = (m_piece == nq) & (m_slot == (source ^ k) * cap + n_slot)
        total += dot(hot(match), ref[:, :piece_cols])
    slot_rows = total.astype(BF16)
    grad_act = jnp.zeros((pad, down.shape[1]), F32)
    for j in range(PIECES):
        grad_act += dot_nt(
            slot_rows[j * pad : (j + 1) * pad], down[0, :, j * piece_cols : (j + 1) * piece_cols]
        )
    gate_pad = dot(hot(iota((pad, slots), 0) == iota((pad, slots), 1)), gate[0, 0])
    grad_up = (grad_act * gate_pad).astype(BF16)
    for j in range(PIECES):
        part = dot_nt(grad_up, up[0, j * piece_cols : (j + 1) * piece_cols, :])
        stack[j * pad : (j + 1) * pad, :] = part.astype(BF16)
    n, m = iota((count, PIECES * pad), 0), iota((count, PIECES * pad), 1)
    nq = quotient(n, cap, count)
    n_slot = n - cap * nq
    m_piece, m_slot = m // pad, m % pad
    for k, ref in enumerate((ret_own, ret_x, ret_y, ret_xy)):
        match = (m_piece == nq) & (m_slot == (source ^ k) * cap + n_slot)
        ref[...] = dot(hot(match), stack[...]).astype(BF16)


def combine_kernel(names, own, from_x, from_y, from_xy, out):
    count, piece_cols = own.shape
    cap = count // PIECES
    tokens = out.shape[1]
    near = (own[...].astype(F32) + from_x[...].astype(F32)).astype(BF16)
    far = (from_y[...].astype(F32) + from_xy[...].astype(F32)).astype(BF16)
    token, lane = iota((tokens, count), 0), iota((tokens, count), 1)
    piece = quotient(lane, cap, count)
    match = [token == names[other : other + 1, :count] for other in range(2)]
    for j in range(PIECES):
        total = dot(hot(match[0] & (piece == j)), near) + dot(hot(match[1] & (piece == j)), far)
        out[0, :, j * piece_cols : (j + 1) * piece_cols] = total.astype(BF16)


def product_kernel(scale, own, from_1, from_2, from_3, after, keep, send):
    count = own.shape[0]
    cap = count // PIECES
    slots = 4 * cap
    half = own.shape[1] - keep.shape[1] // 2
    piece_cols = own.shape[1] - half
    _, _, _, _, core = place()
    refs = (own, from_1, from_2, from_3)
    rows = jnp.concatenate([ref[:, :piece_cols].astype(F32) for ref in refs], 0).astype(BF16)
    m, n = iota((4 * count, count), 0), iota((4 * count, count), 1)
    mq = quotient(m, cap, 4 * count)
    m_slot = m - cap * mq
    m_part, m_loc, m_source, m_has = mq >> 4, (mq >> 3) & 1, (mq >> 1) & 3, mq & 1
    nq = quotient(n, cap, count)
    n_loc, n_row = nq >> 2, n - slots * (nq >> 2)
    ok = (m_has == m_part) & (m_loc == n_loc) & (m_source * cap + m_slot == n_row)
    place_rows = jnp.where(ok, scale, 0.0).astype(BF16)
    spread = [dot(place_rows, ref[:, piece_cols:]) for ref in refs]
    rows_dev = half // 4
    for part in range(2):
        for loc in range(2):
            at = (2 * part + loc) * count
            hidden = jnp.concatenate([value[at : at + count] for value in spread], 0)
            product = dot(hidden.T.astype(BF16), rows)
            for zb in range(2):
                base = zb * 2 * rows_dev
                first = product[base : base + rows_dev]
                second = product[base + rows_dev : base + 2 * rows_dev]
                block = slice((2 * loc + zb) * rows_dev, (2 * loc + zb + 1) * rows_dev)
                cols = slice(part * piece_cols, (part + 1) * piece_cols)
                keep[block, cols] = jnp.where(core == 0, first, second).astype(BF16)
                send[block, cols] = jnp.where(core == 0, second, first).astype(BF16)


def add_kernel(mine, other, own, to_x, to_z, to_xz):
    rows_dev = own.shape[0]
    _, loc, zb, _, _ = place()
    for k, out in enumerate((own, to_z, to_x, to_xz)):
        at = pl.ds(pl.multiple_of(((2 * loc + zb) ^ k) * rows_dev, rows_dev), rows_dev)
        out[...] = (mine[at, :].astype(F32) + other[at, :].astype(F32)).astype(BF16)


def join_kernel(own, from_x, from_z, from_xz, out):
    cols = own.shape[1]
    _, loc, zb, _, _ = place()
    for k, ref in enumerate((own, from_z, from_x, from_xz)):
        at = pl.ds(pl.multiple_of(((2 * loc + zb) ^ k) * cols, cols), cols)
        out[0, :, at] = ref[...].astype(F32)


VM = pl.BlockSpec(memory_space=pltpu.VMEM)
ANY = pl.BlockSpec(memory_space=pl.ANY)


def call(kernel, outs, args, specs=None, scratch=(), flops=0, nbytes=0):
    out_shape = tuple(jax.ShapeDtypeStruct(shape, dtype) for shape, dtype in outs)
    result = pl.pallas_call(
        kernel,
        out_shape=out_shape,
        in_specs=specs or [VM] * len(args),
        out_specs=tuple([VM] * len(outs)),
        scratch_shapes=list(scratch),
        compiler_params=pltpu.CompilerParams(vmem_limit_bytes=16 * 1024 * 1024),
        cost_estimate=pl.CostEstimate(flops=flops, bytes_accessed=nbytes, transcendentals=0),
    )(*args)
    return result


def hbm(value):
    return pltpu.with_memory_space_constraint(value, pltpu.HBM)


def swap(value, group_flip=0, loc_flip=0, dp_flip=0):
    sizes = [lax.axis_size(axis) for axis in AXES]
    pairs = []
    for g in range(sizes[0]):
        for l in range(sizes[1]):
            for d in range(sizes[2]):
                here = (g * sizes[1] + l) * sizes[2] + d
                there = ((g ^ group_flip) * sizes[1] + (l ^ loc_flip)) * sizes[2] + (d ^ dp_flip)
                pairs.append((here, there))
    return lax.ppermute(value, AXES, pairs)


def local_messages(
    out_grad, slot_token, slot_count, slot_weight, up_weight, down_weight, hidden_saved, gate_saved
):
    model = out_grad.shape[2]
    tokens = out_grad.shape[1]
    cap = slot_token.shape[3]
    hidden_dev = hidden_saved.shape[3]
    replicas = lax.axis_size("dp")
    piece_cols, half, count = model // PIECES, hidden_dev // 2, PIECES * cap
    rows_dev = hidden_dev // replicas
    inputs = (slot_token, slot_count, slot_weight, out_grad, hidden_saved)
    spaces = (pltpu.SMEM, pltpu.SMEM, pltpu.VMEM, pltpu.VMEM, pltpu.VMEM)
    near, far, names = call(
        select_kernel,
        [
            ((count, piece_cols + half), BF16),
            ((count, piece_cols), BF16),
            ((8, 128), jnp.int32),
        ],
        [hbm(x) for x in inputs],
        [ANY] * 5,
        scratch=[space(x.shape, x.dtype) for space, x in zip(spaces, inputs)]
        + [pltpu.SemaphoreType.DMA((5,))],
        nbytes=tokens * model * 2,
    )
    from_x = swap(near, loc_flip=1)
    from_y = swap(far, group_flip=1)
    from_xy = swap(far, group_flip=1, loc_flip=1)
    arrived = (near, from_x, from_y, from_xy)
    held = (down_weight, up_weight, gate_saved)
    down, up, gate = call(
        load_kernel,
        [(x.shape, x.dtype) for x in held],
        [hbm(x) for x in held] + [far],
        [ANY] * 4,
        scratch=[pltpu.SemaphoreType.DMA((3,))],
        nbytes=8 * model * hidden_dev,
    )
    message = ((count, piece_cols + half), BF16)
    mine, to_1, to_2, to_3 = call(
        spread_kernel, [message] * 4, arrived + (gate,), [VM] * 4 + [ANY], nbytes=count * model
    )
    from_1 = swap(to_1, dp_flip=2)
    from_2 = swap(to_2, dp_flip=4)
    from_3 = swap(to_3, dp_flip=6)
    pad = -(-4 * cap // 16) * 16
    ret_own, ret_x, ret_y, ret_xy = call(
        expert_kernel,
        [((count, piece_cols), BF16)] * 4,
        arrived + (down, gate, up),
        scratch=[pltpu.VMEM((PIECES * pad, piece_cols), BF16)],
        flops=4 * pad * model * hidden_dev,
        nbytes=4 * model * hidden_dev,
    )
    back_x = swap(ret_x, loc_flip=1)
    back_y = swap(ret_y, group_flip=1)
    back_xy = swap(ret_xy, group_flip=1, loc_flip=1)
    (input_grad,) = call(
        combine_kernel,
        [((1, tokens, model), BF16)],
        (names, ret_own, back_x, back_y, back_xy),
        nbytes=2 * tokens * model,
    )
    block = ((4 * rows_dev, 2 * piece_cols), BF16)
    keep, send = call(
        functools.partial(product_kernel, 1.0 / replicas),
        [block] * 2,
        (mine, from_1, from_2, from_3, ret_own),
        [VM] * 4 + [ANY],
        nbytes=16 * rows_dev * piece_cols,
    )
    other = swap(send, dp_flip=1)
    block = ((rows_dev, 2 * piece_cols), BF16)
    own, to_x, to_z, to_xz = call(add_kernel, [block] * 4, (keep, other), nbytes=1 << 20)
    got_x = swap(to_x, loc_flip=1)
    got_z = swap(to_z, dp_flip=2)
    got_xz = swap(to_xz, loc_flip=1, dp_flip=2)
    (down_grad,) = call(
        join_kernel, [((1, rows_dev, model), F32)], (own, got_x, got_z, got_xz), nbytes=1 << 20
    )
    return (input_grad, down_grad)


def local(*args):
    sizes = tuple(lax.axis_size(axis) for axis in AXES)
    model, cap, hidden_dev = args[0].shape[2], args[1].shape[3], args[6].shape[3]
    fits = sizes == (2, 2, 8) and model % (PIECES * 128) == 0
    fits = fits and hidden_dev % 256 == 0 and args[0].shape[1] % 16 == 0 and 4 * cap <= 32
    return (local_messages if fits else local_collectives)(*args)


def solution(mesh):
    return jax.shard_map(
        local,
        mesh=mesh,
        in_specs=(
            P("dp", ("grp", "loc"), None),
            P("dp", ("grp", "loc"), None, None),
            P("dp", ("grp", "loc"), None),
            P("dp", ("grp", "loc"), None, None),
            P("grp", None, "loc"),
            P("grp", "loc", None),
            P("dp", "grp", None, "loc"),
            P("dp", "grp", None, "loc"),
        ),
        out_specs=(P("dp", ("grp", "loc"), None), P("grp", ("loc", "dp"), None)),
        check_vma=False,
    )
```

```python
import functools

import jax
import jax.numpy as jnp
from jax import lax
from jax.experimental import pallas as pl
from jax.experimental.pallas import tpu as pltpu
from jax.sharding import PartitionSpec as P

AXES = ("grp", "loc", "dp")
PIECES = 8
F32 = jnp.float32
BF16 = jnp.bfloat16


def local_collectives(
    out_grad, slot_token, slot_count, slot_weight, up_weight, down_weight, hidden_saved, gate_saved
):
    group_count = lax.axis_size("grp")
    local_count = lax.axis_size("loc")
    replicas = lax.axis_size("dp")
    grad_rows = out_grad[0]
    tok_dev = grad_rows.shape[0]
    model_dim = grad_rows.shape[1]
    tokens = slot_token[0, 0]
    capacity = tokens.shape[1]
    live_mask = jnp.arange(capacity, dtype=jnp.int32)[None, :] < slot_count[0, 0][:, None]
    picked = jnp.take(grad_rows, tokens.reshape(-1), axis=0).reshape(
        group_count, capacity, model_dim
    )
    outgoing = jnp.where(live_mask[:, :, None], picked, jnp.zeros((), jnp.bfloat16))
    weights = slot_weight[0, 0]
    arrived, arrived_weights = (
        lax.all_to_all(outgoing, "grp", split_axis=0, concat_axis=0, tiled=True),
        lax.all_to_all(weights, "grp", split_axis=0, concat_axis=0, tiled=True),
    )
    rows_all, weights_all = (
        lax.all_gather(arrived[:, None], "loc", axis=1, tiled=True),
        lax.all_gather(arrived_weights[:, None], "loc", axis=1, tiled=True),
    )
    slot_total = group_count * local_count * capacity
    slot_rows = rows_all.reshape(slot_total, model_dim)
    slot_scale = weights_all.reshape(slot_total).astype(jnp.float32)[:, None]
    hidden = hidden_saved[0, 0]
    gate_act = gate_saved[0, 0]
    w_down = down_weight[0]
    w_up = up_weight[0]
    grad_act = lax.dot_general(
        slot_rows, w_down, (((1,), (1,)), ((), ())), preferred_element_type=jnp.float32
    )
    grad_up = (slot_scale * grad_act * gate_act.astype(jnp.float32)).astype(jnp.bfloat16)
    partial_value = lax.dot_general(
        grad_up, w_up, (((1,), (1,)), ((), ())), preferred_element_type=jnp.float32
    )
    partial_value = partial_value.astype(jnp.bfloat16)
    weighted = (slot_scale * hidden.astype(jnp.float32)).astype(jnp.bfloat16)
    product = lax.dot_general(
        weighted, slot_rows, (((0,), (0,)), ((), ())), preferred_element_type=jnp.float32
    )
    rounded = lax.optimization_barrier(product.astype(jnp.bfloat16))
    summed = lax.psum_scatter(
        rounded.astype(jnp.float32).astype(jnp.bfloat16), "dp", scatter_dimension=0, tiled=True
    ).astype(jnp.float32)
    down_grad = (summed / replicas)[None]
    term_rows = lax.optimization_barrier(partial_value).astype(jnp.float32)
    term_rows = term_rows.reshape(group_count, local_count, capacity, model_dim)
    summed_rows = lax.psum_scatter(
        term_rows.astype(jnp.bfloat16), "loc", scatter_dimension=1, tiled=True
    )
    returned = lax.all_to_all(summed_rows, "grp", split_axis=0, concat_axis=0, tiled=True)
    contribs = returned.reshape(group_count * capacity, model_dim)
    matches = jnp.arange(tok_dev, dtype=jnp.int32)[:, None] == tokens.reshape(-1)[None, :]
    onehot = (matches & live_mask.reshape(-1)[None, :]).astype(jnp.bfloat16)
    input_grad = jnp.dot(onehot, contribs, preferred_element_type=jnp.float32).astype(jnp.bfloat16)[
        None
    ]
    return (input_grad, down_grad)


def iota(shape, dim):
    return lax.broadcasted_iota(jnp.int32, shape, dim)


def quotient(value, cap, most):
    shift = 16
    factor = (1 << shift) // cap + 1
    assert all((v * factor) >> shift == v // cap for v in range(most))
    return lax.shift_right_logical(value * factor, shift)


def dot(a, b):
    return jnp.dot(a, b, preferred_element_type=F32)


def dot_nt(a, b):
    return lax.dot_general(a, b, (((1,), (1,)), ((), ())), preferred_element_type=F32)


def hot(condition):
    return jnp.where(condition, 1.0, 0.0).astype(BF16)


def place():
    group, loc, dp = (lax.axis_index(axis) for axis in AXES)
    z = dp // 2
    return group, loc, z % 2, z // 2, dp % 2


def select_kernel(
    tok_hbm, cnt_hbm, weight_hbm, rows_hbm, hidden_hbm, near, far, names, tok, cnt, weight, rows,
    hidden, sems
):
    pairs = (
        (tok_hbm, tok), (cnt_hbm, cnt), (weight_hbm, weight), (rows_hbm, rows), (hidden_hbm, hidden)
    )
    copies = [pltpu.make_async_copy(a, b, sems.at[i]) for i, (a, b) in enumerate(pairs)]
    for copy in copies:
        copy.start()
    cap = tok.shape[3]
    group, _, _, _, _ = place()
    tokens, model = rows.shape[1], rows.shape[2]
    piece_cols = model // PIECES
    count = PIECES * cap
    row, token = iota((count, tokens), 0), iota((count, tokens), 1)
    piece = quotient(row, cap, count)
    slot = row - cap * piece
    line, lane = iota(names.shape, 0), iota(names.shape, 1)
    lane_slot = lane - cap * quotient(lane, cap, names.shape[1])
    for copy in copies[:3]:
        copy.wait()
    scale = weight[0, 0].astype(F32)
    named = jnp.full(names.shape, -1, jnp.int32)
    values = []
    for other in range(2):
        expert = jnp.where(group == other, 0, 1)
        live = cnt[0, 0, expert]
        value = jnp.zeros((count, tokens), F32)
        for s in range(cap):
            name = jnp.where(s < live, tok[0, 0, expert, s], -1)
            factor = jnp.where(
                expert == 0, scale[0:1, s : s + 1], scale[1:2, s : s + 1]
            )
            value = jnp.where((slot == s) & (token == name), factor, value)
            named = jnp.where((line == other) & (lane_slot == s), name, named)
        values.append(value)
    names[...] = named
    for copy in copies[3:]:
        copy.wait()
    for value, out in zip(values, (near, far)):
        total = jnp.zeros((count, piece_cols), F32)
        for j in range(PIECES):
            chosen = jnp.where(piece == j, value, 0.0).astype(BF16)
            total += dot(chosen, rows[0, :, j * piece_cols : (j + 1) * piece_cols])
        out[:, :piece_cols] = total.astype(BF16)
    half = hidden.shape[3] // 2
    slots = hidden.shape[2]
    r, c = iota((count, slots), 0), iota((count, slots), 1)
    folded = dot(hot(r == c), hidden[0, 0, :, :half]) + dot(
        hot(r == c + slots), hidden[0, 0, :, half:]
    )
    near[:, piece_cols:] = folded.astype(BF16)


def load_kernel(down_hbm, up_hbm, gate_hbm, after, down, up, gate, sems):
    pairs = ((down_hbm, down), (up_hbm, up), (gate_hbm, gate))
    copies = [pltpu.make_async_copy(a, b, sems.at[i]) for i, (a, b) in enumerate(pairs)]
    for copy in copies:
        copy.start()
    for copy in copies:
        copy.wait()


def spread_kernel(own, from_x, from_y, from_xy, after, keep, to_1, to_2, to_3):
    count, piece_cols = from_y.shape
    cap = count // PIECES
    slots = 4 * cap
    group, loc, zb, pair, _ = place()
    source = 2 * group + loc
    m, n = iota((2 * count, count), 0), iota((2 * count, count), 1)
    mq, nq = quotient(m, cap, 2 * count), quotient(n, cap, count)
    m_slot, n_slot = m - cap * mq, n - cap * nq
    m_flip, m_source, m_part = mq >> 3, (mq >> 1) & 3, mq & 1
    wanted = 4 * loc + 2 * (zb ^ m_flip) + m_part
    rows_ok = (m_slot == n_slot) & (nq == wanted)
    total = jnp.zeros((2 * count, piece_cols), F32)
    for k, ref in enumerate((own, from_x, from_y, from_xy)):
        total += dot(hot(rows_ok & (m_source == (source ^ k))), ref[:, :piece_cols])
    m_loc, m_row = (mq >> 2) & 1, m - slots * (mq >> 2)
    n_half, n_row = nq >> 2, n - slots * (nq >> 2)
    hidden_ok = (m_row == n_row) & (n_half == (pair ^ m_flip))
    hidden = dot(hot(hidden_ok & (m_loc == loc)), own[:, piece_cols:]) + dot(
        hot(hidden_ok & (m_loc != loc)), from_x[:, piece_cols:]
    )
    total, hidden = total.astype(BF16), hidden.astype(BF16)
    for ref, flip_zb, flip_pair in ((keep, 0, 0), (to_1, 1, 0), (to_2, 0, 1), (to_3, 1, 1)):
        ref[:, :piece_cols] = total[flip_zb * count : (flip_zb + 1) * count]
        ref[:, piece_cols:] = hidden[flip_pair * count : (flip_pair + 1) * count]


def expert_kernel(
    own, from_x, from_y, from_xy, down, gate, up, ret_own, ret_y, ret_x, stack
):
    count, piece_cols = from_y.shape
    cap = count // PIECES
    pad = stack.shape[0] // PIECES
    slots = gate.shape[2]
    group, loc, _, _, _ = place()
    source = 2 * group + loc
    m, n = iota((PIECES * pad, count), 0), iota((PIECES * pad, count), 1)
    nq = quotient(n, cap, count)
    n_slot = n - cap * nq
    m_piece, m_slot = m // pad, m % pad
    total = jnp.zeros((PIECES * pad, piece_cols), F32)
    for k, ref in enumerate((own, from_x, from_y, from_xy)):
        match = (m_piece == nq) & (m_slot == (source ^ k) * cap + n_slot)
        total += dot(hot(match), ref[:, :piece_cols])
    slot_rows = total.astype(BF16)
    grad_act = jnp.zeros((pad, down.shape[1]), F32)
    for j in range(PIECES):
        grad_act += dot_nt(
            slot_rows[j * pad : (j + 1) * pad], down[0, :, j * piece_cols : (j + 1) * piece_cols]
        )
    gate_pad = dot(hot(iota((pad, slots), 0) == iota((pad, slots), 1)), gate[0, 0])
    grad_up = (grad_act * gate_pad).astype(BF16)
    for j in range(PIECES):
        part = dot_nt(grad_up, up[0, j * piece_cols : (j + 1) * piece_cols, :])
        stack[j * pad : (j + 1) * pad, :] = part.astype(BF16)
    n, m = iota((count, PIECES * pad), 0), iota((count, PIECES * pad), 1)
    nq = quotient(n, cap, count)
    n_slot = n - cap * nq
    m_piece, m_slot = m // pad, m % pad
    back = []
    for k in range(4):
        match = (m_piece == nq) & (m_slot == (source ^ k) * cap + n_slot)
        back.append(dot(hot(match), stack[...]))
    ret_own[...] = back[0].astype(BF16)
    ret_y[...] = back[2].astype(BF16)
    ret_x[...] = jnp.concatenate([back[1], back[3]], 0).astype(BF16)


def merge_kernel(ret_own, ret_y, from_x, near, far):
    other = from_x[...].astype(F32)
    count = near.shape[0]
    near[...] = (ret_own[...].astype(F32) + other[:count]).astype(BF16)
    far[...] = (ret_y[...].astype(F32) + other[count:]).astype(BF16)


def product_kernel(scale, own, from_2, from_3, from_1, after, keep, send):
    count = own.shape[0]
    cap = count // PIECES
    slots = 4 * cap
    half = own.shape[1] - keep.shape[1] // 2
    piece_cols = own.shape[1] - half
    _, _, _, _, core = place()
    refs = (own, from_1, from_2, from_3)
    rows = jnp.concatenate([ref[:, :piece_cols].astype(F32) for ref in refs], 0).astype(BF16)
    m, n = iota((4 * count, count), 0), iota((4 * count, count), 1)
    mq = quotient(m, cap, 4 * count)
    m_slot = m - cap * mq
    m_part, m_loc, m_source, m_has = mq >> 4, (mq >> 3) & 1, (mq >> 1) & 3, mq & 1
    nq = quotient(n, cap, count)
    n_loc, n_row = nq >> 2, n - slots * (nq >> 2)
    ok = (m_has == m_part) & (m_loc == n_loc) & (m_source * cap + m_slot == n_row)
    place_rows = jnp.where(ok, scale, 0.0).astype(BF16)
    spread = [dot(place_rows, ref[:, piece_cols:]) for ref in refs]
    rows_dev = half // 4
    for part in range(2):
        for loc in range(2):
            at = (2 * part + loc) * count
            hidden = jnp.concatenate([value[at : at + count] for value in spread], 0)
            product = dot(hidden.T.astype(BF16), rows)
            for zb in range(2):
                base = zb * 2 * rows_dev
                first = product[base : base + rows_dev]
                second = product[base + rows_dev : base + 2 * rows_dev]
                block = slice((2 * loc + zb) * rows_dev, (2 * loc + zb + 1) * rows_dev)
                cols = slice(part * piece_cols, (part + 1) * piece_cols)
                keep[block, cols] = jnp.where(core == 0, first, second).astype(BF16)
                send[block, cols] = jnp.where(core == 0, second, first).astype(BF16)


def add_kernel(mine, other, own, to_x, to_z, to_xz):
    rows_dev = own.shape[0]
    _, loc, zb, _, _ = place()
    for k, out in enumerate((own, to_z, to_x, to_xz)):
        at = pl.ds(pl.multiple_of(((2 * loc + zb) ^ k) * rows_dev, rows_dev), rows_dev)
        out[...] = (mine[at, :].astype(F32) + other[at, :].astype(F32)).astype(BF16)


def finish_kernel(
    own, from_x, from_z, from_xz, names, near, far, tokens_hbm, down_hbm, tokens_out, down_out, sems
):
    cols = own.shape[1]
    count, piece_cols = near.shape
    cap = count // PIECES
    tokens = tokens_out.shape[1]
    _, loc, zb, _, _ = place()
    copies = []

    def send(source, target):
        copy = pltpu.make_async_copy(source, target, sems.at[len(copies)])
        copy.start()
        copies.append(copy)

    for k, ref in enumerate((own, from_z, from_x, from_xz)):
        start = pl.multiple_of(((2 * loc + zb) ^ k) * cols, cols)
        down_out[k] = ref[...].astype(F32)
        send(down_out.at[k], down_hbm.at[0, :, pl.ds(start, cols)])
    token, lane = iota((tokens, count), 0), iota((tokens, count), 1)
    piece = quotient(lane, cap, count)
    match = [token == names[other : other + 1, :count] for other in range(2)]
    for j in range(PIECES):
        total = dot(hot(match[0] & (piece == j)), near[...]) + dot(
            hot(match[1] & (piece == j)), far[...]
        )
        tokens_out[j] = total.astype(BF16)
        send(tokens_out.at[j], tokens_hbm.at[0, :, pl.ds(j * piece_cols, piece_cols)])
    for copy in copies:
        copy.wait()


VM = pl.BlockSpec(memory_space=pltpu.VMEM)
ANY = pl.BlockSpec(memory_space=pl.ANY)


def call(kernel, outs, args, specs=None, outs_specs=None, scratch=(), flops=0, nbytes=0):
    out_shape = tuple(jax.ShapeDtypeStruct(shape, dtype) for shape, dtype in outs)
    result = pl.pallas_call(
        kernel,
        out_shape=out_shape,
        in_specs=specs or [VM] * len(args),
        out_specs=tuple(outs_specs or [VM] * len(outs)),
        scratch_shapes=list(scratch),
        compiler_params=pltpu.CompilerParams(vmem_limit_bytes=16 * 1024 * 1024),
        cost_estimate=pl.CostEstimate(flops=flops, bytes_accessed=nbytes, transcendentals=0),
    )(*args)
    return result


def hbm(value):
    return pltpu.with_memory_space_constraint(value, pltpu.HBM)


def swap(value, group_flip=0, loc_flip=0, dp_flip=0):
    sizes = [lax.axis_size(axis) for axis in AXES]
    pairs = []
    for g in range(sizes[0]):
        for l in range(sizes[1]):
            for d in range(sizes[2]):
                here = (g * sizes[1] + l) * sizes[2] + d
                there = ((g ^ group_flip) * sizes[1] + (l ^ loc_flip)) * sizes[2] + (d ^ dp_flip)
                pairs.append((here, there))
    return lax.ppermute(value, AXES, pairs)


def local_messages(
    out_grad, slot_token, slot_count, slot_weight, up_weight, down_weight, hidden_saved, gate_saved
):
    model = out_grad.shape[2]
    tokens = out_grad.shape[1]
    cap = slot_token.shape[3]
    hidden_dev = hidden_saved.shape[3]
    replicas = lax.axis_size("dp")
    piece_cols, half, count = model // PIECES, hidden_dev // 2, PIECES * cap
    rows_dev = hidden_dev // replicas
    inputs = (slot_token, slot_count, slot_weight, out_grad, hidden_saved)
    spaces = (pltpu.SMEM, pltpu.SMEM, pltpu.VMEM, pltpu.VMEM, pltpu.VMEM)
    near, far, names = call(
        select_kernel,
        [
            ((count, piece_cols + half), BF16),
            ((count, piece_cols), BF16),
            ((8, 128), jnp.int32),
        ],
        [hbm(x) for x in inputs],
        [ANY] * 5,
        scratch=[space(x.shape, x.dtype) for space, x in zip(spaces, inputs)]
        + [pltpu.SemaphoreType.DMA((5,))],
        nbytes=tokens * model * 2,
    )
    from_xy = swap(far, group_flip=1, loc_flip=1)
    from_y = swap(far, group_flip=1)
    from_x = swap(near, loc_flip=1)
    arrived = (near, from_x, from_y, from_xy)
    held = (down_weight, up_weight, gate_saved)
    down, up, gate = call(
        load_kernel,
        [(x.shape, x.dtype) for x in held],
        [hbm(x) for x in held] + [far],
        [ANY] * 4,
        scratch=[pltpu.SemaphoreType.DMA((3,))],
        nbytes=8 * model * hidden_dev,
    )
    message = ((count, piece_cols + half), BF16)
    mine, to_1, to_2, to_3 = call(
        spread_kernel, [message] * 4, arrived + (gate,), [VM] * 4 + [ANY], nbytes=count * model
    )
    from_2 = swap(to_2, dp_flip=4)
    from_3 = swap(to_3, dp_flip=6)
    from_1 = swap(to_1, dp_flip=2)
    pad = -(-4 * cap // 16) * 16
    part = ((count, piece_cols), BF16)
    ret_own, ret_y, ret_x = call(
        expert_kernel,
        [part, part, ((2 * count, piece_cols), BF16)],
        arrived + (down, gate, up),
        scratch=[pltpu.VMEM((PIECES * pad, piece_cols), BF16)],
        flops=4 * pad * model * hidden_dev,
        nbytes=4 * model * hidden_dev,
    )
    back_x = swap(ret_x, loc_flip=1)
    near_sum, far_sum = call(merge_kernel, [part] * 2, (ret_own, ret_y, back_x), nbytes=1 << 18)
    back_y = swap(far_sum, group_flip=1)
    block = ((4 * rows_dev, 2 * piece_cols), BF16)
    keep, send = call(
        functools.partial(product_kernel, 1.0 / replicas),
        [block] * 2,
        (mine, from_2, from_3, from_1, ret_own),
        [VM] * 4 + [ANY],
        nbytes=16 * rows_dev * piece_cols,
    )
    other = swap(send, dp_flip=1)
    block = ((rows_dev, 2 * piece_cols), BF16)
    own, to_x, to_z, to_xz = call(add_kernel, [block] * 4, (keep, other), nbytes=1 << 20)
    got_xz = swap(to_xz, loc_flip=1, dp_flip=2)
    got_z = swap(to_z, dp_flip=2)
    got_x = swap(to_x, loc_flip=1)
    input_grad, down_grad = call(
        finish_kernel,
        [((1, tokens, model), BF16), ((1, rows_dev, model), F32)],
        (own, got_x, got_z, got_xz, names, near_sum, back_y),
        outs_specs=[ANY] * 2,
        scratch=[
            pltpu.VMEM((PIECES, tokens, piece_cols), BF16),
            pltpu.VMEM((4, rows_dev, 2 * piece_cols), F32),
            pltpu.SemaphoreType.DMA((4 + PIECES,)),
        ],
        nbytes=4 << 20,
    )
    return (input_grad, down_grad)


def local(*args):
    sizes = tuple(lax.axis_size(axis) for axis in AXES)
    model, cap, hidden_dev = args[0].shape[2], args[1].shape[3], args[6].shape[3]
    fits = sizes == (2, 2, 8) and model % (PIECES * 128) == 0
    fits = fits and hidden_dev % 256 == 0 and args[0].shape[1] % 16 == 0 and 4 * cap <= 32
    return (local_messages if fits else local_collectives)(*args)


def solution(mesh):
    return jax.shard_map(
        local,
        mesh=mesh,
        in_specs=(
            P("dp", ("grp", "loc"), None),
            P("dp", ("grp", "loc"), None, None),
            P("dp", ("grp", "loc"), None),
            P("dp", ("grp", "loc"), None, None),
            P("grp", None, "loc"),
            P("grp", "loc", None),
            P("dp", "grp", None, "loc"),
            P("dp", "grp", None, "loc"),
        ),
        out_specs=(P("dp", ("grp", "loc"), None), P("grp", ("loc", "dp"), None)),
        check_vma=False,
    )
```

```python
import functools

import jax
import jax.numpy as jnp
from jax import lax
from jax.experimental import pallas as pl
from jax.experimental.pallas import tpu as pltpu
from jax.sharding import PartitionSpec as P

AXES = ("grp", "loc", "dp")
PIECES = 8
F32 = jnp.float32
BF16 = jnp.bfloat16


def local_collectives(
    out_grad, slot_token, slot_count, slot_weight, up_weight, down_weight, hidden_saved, gate_saved
):
    group_count = lax.axis_size("grp")
    local_count = lax.axis_size("loc")
    replicas = lax.axis_size("dp")
    grad_rows = out_grad[0]
    tok_dev = grad_rows.shape[0]
    model_dim = grad_rows.shape[1]
    tokens = slot_token[0, 0]
    capacity = tokens.shape[1]
    live_mask = jnp.arange(capacity, dtype=jnp.int32)[None, :] < slot_count[0, 0][:, None]
    picked = jnp.take(grad_rows, tokens.reshape(-1), axis=0).reshape(
        group_count, capacity, model_dim
    )
    outgoing = jnp.where(live_mask[:, :, None], picked, jnp.zeros((), jnp.bfloat16))
    weights = slot_weight[0, 0]
    arrived, arrived_weights = (
        lax.all_to_all(outgoing, "grp", split_axis=0, concat_axis=0, tiled=True),
        lax.all_to_all(weights, "grp", split_axis=0, concat_axis=0, tiled=True),
    )
    rows_all, weights_all = (
        lax.all_gather(arrived[:, None], "loc", axis=1, tiled=True),
        lax.all_gather(arrived_weights[:, None], "loc", axis=1, tiled=True),
    )
    slot_total = group_count * local_count * capacity
    slot_rows = rows_all.reshape(slot_total, model_dim)
    slot_scale = weights_all.reshape(slot_total).astype(jnp.float32)[:, None]
    hidden = hidden_saved[0, 0]
    gate_act = gate_saved[0, 0]
    w_down = down_weight[0]
    w_up = up_weight[0]
    grad_act = lax.dot_general(
        slot_rows, w_down, (((1,), (1,)), ((), ())), preferred_element_type=jnp.float32
    )
    grad_up = (slot_scale * grad_act * gate_act.astype(jnp.float32)).astype(jnp.bfloat16)
    partial_value = lax.dot_general(
        grad_up, w_up, (((1,), (1,)), ((), ())), preferred_element_type=jnp.float32
    )
    partial_value = partial_value.astype(jnp.bfloat16)
    weighted = (slot_scale * hidden.astype(jnp.float32)).astype(jnp.bfloat16)
    product = lax.dot_general(
        weighted, slot_rows, (((0,), (0,)), ((), ())), preferred_element_type=jnp.float32
    )
    rounded = lax.optimization_barrier(product.astype(jnp.bfloat16))
    summed = lax.psum_scatter(
        rounded.astype(jnp.float32).astype(jnp.bfloat16), "dp", scatter_dimension=0, tiled=True
    ).astype(jnp.float32)
    down_grad = (summed / replicas)[None]
    term_rows = lax.optimization_barrier(partial_value).astype(jnp.float32)
    term_rows = term_rows.reshape(group_count, local_count, capacity, model_dim)
    summed_rows = lax.psum_scatter(
        term_rows.astype(jnp.bfloat16), "loc", scatter_dimension=1, tiled=True
    )
    returned = lax.all_to_all(summed_rows, "grp", split_axis=0, concat_axis=0, tiled=True)
    contribs = returned.reshape(group_count * capacity, model_dim)
    matches = jnp.arange(tok_dev, dtype=jnp.int32)[:, None] == tokens.reshape(-1)[None, :]
    onehot = (matches & live_mask.reshape(-1)[None, :]).astype(jnp.bfloat16)
    input_grad = jnp.dot(onehot, contribs, preferred_element_type=jnp.float32).astype(jnp.bfloat16)[
        None
    ]
    return (input_grad, down_grad)


def iota(shape, dim):
    return lax.broadcasted_iota(jnp.int32, shape, dim)


def quotient(value, cap, most):
    shift = 16
    factor = (1 << shift) // cap + 1
    assert all((v * factor) >> shift == v // cap for v in range(most))
    return lax.shift_right_logical(value * factor, shift)


def dot(a, b):
    return jnp.dot(a, b, preferred_element_type=F32)


def dot_nt(a, b):
    return lax.dot_general(a, b, (((1,), (1,)), ((), ())), preferred_element_type=F32)


def hot(condition):
    return jnp.where(condition, 1.0, 0.0).astype(BF16)


def place():
    group, loc, dp = (lax.axis_index(axis) for axis in AXES)
    z = dp // 2
    return group, loc, z % 2, z // 2, dp % 2


def select_kernel(
    tok_hbm, cnt_hbm, weight_hbm, rows_hbm, hidden_hbm, near, far, names, tok, cnt, weight, rows,
    hidden, sems
):
    pairs = (
        (tok_hbm, tok), (cnt_hbm, cnt), (weight_hbm, weight), (rows_hbm, rows), (hidden_hbm, hidden)
    )
    copies = [pltpu.make_async_copy(a, b, sems.at[i]) for i, (a, b) in enumerate(pairs)]
    for copy in copies:
        copy.start()
    cap = tok.shape[3]
    group, _, _, _, _ = place()
    tokens, model = rows.shape[1], rows.shape[2]
    piece_cols = model // PIECES
    count = PIECES * cap
    row, token = iota((count, tokens), 0), iota((count, tokens), 1)
    piece = quotient(row, cap, count)
    slot = row - cap * piece
    line, lane = iota(names.shape, 0), iota(names.shape, 1)
    lane_slot = lane - cap * quotient(lane, cap, names.shape[1])
    for copy in copies[:3]:
        copy.wait()
    scale = weight[0, 0].astype(F32)
    named = jnp.full(names.shape, -1, jnp.int32)
    values = []
    for other in range(2):
        expert = jnp.where(group == other, 0, 1)
        live = cnt[0, 0, expert]
        value = jnp.zeros((count, tokens), F32)
        for s in range(cap):
            name = jnp.where(s < live, tok[0, 0, expert, s], -1)
            factor = jnp.where(
                expert == 0, scale[0:1, s : s + 1], scale[1:2, s : s + 1]
            )
            value = jnp.where((slot == s) & (token == name), factor, value)
            named = jnp.where((line == other) & (lane_slot == s), name, named)
        values.append(value)
    names[...] = named
    for copy in copies[3:]:
        copy.wait()
    value = jnp.concatenate(values, 0)
    piece = jnp.concatenate([piece, piece], 0)
    total = jnp.zeros((2 * count, piece_cols), F32)
    for j in range(PIECES):
        chosen = jnp.where(piece == j, value, 0.0).astype(BF16)
        total += dot(chosen, rows[0, :, j * piece_cols : (j + 1) * piece_cols])
    near[:, :piece_cols] = total[:count].astype(BF16)
    far[...] = total[count:].astype(BF16)
    half = hidden.shape[3] // 2
    slots = hidden.shape[2]
    r, c = iota((count, slots), 0), iota((count, slots), 1)
    folded = dot(hot(r == c), hidden[0, 0, :, :half]) + dot(
        hot(r == c + slots), hidden[0, 0, :, half:]
    )
    near[:, piece_cols:] = folded.astype(BF16)


def load_kernel(down_hbm, up_hbm, gate_hbm, after, down, up, gate, sems):
    pairs = ((down_hbm, down), (up_hbm, up), (gate_hbm, gate))
    copies = [pltpu.make_async_copy(a, b, sems.at[i]) for i, (a, b) in enumerate(pairs)]
    for copy in copies:
        copy.start()
    for copy in copies:
        copy.wait()


def spread_kernel(own, from_x, from_y, from_xy, after, keep, to_1, to_2, to_3):
    count, piece_cols = from_y.shape
    cap = count // PIECES
    slots = 4 * cap
    group, loc, zb, pair, _ = place()
    source = 2 * group + loc
    m, n = iota((2 * count, count), 0), iota((2 * count, count), 1)
    mq, nq = quotient(m, cap, 2 * count), quotient(n, cap, count)
    m_slot, n_slot = m - cap * mq, n - cap * nq
    m_flip, m_source, m_part = mq >> 3, (mq >> 1) & 3, mq & 1
    wanted = 4 * loc + 2 * (zb ^ m_flip) + m_part
    rows_ok = (m_slot == n_slot) & (nq == wanted)
    total = jnp.zeros((2 * count, piece_cols), F32)
    for k, ref in enumerate((own, from_x, from_y, from_xy)):
        total += dot(hot(rows_ok & (m_source == (source ^ k))), ref[:, :piece_cols])
    m_loc, m_row = (mq >> 2) & 1, m - slots * (mq >> 2)
    n_half, n_row = nq >> 2, n - slots * (nq >> 2)
    hidden_ok = (m_row == n_row) & (n_half == (pair ^ m_flip))
    hidden = dot(hot(hidden_ok & (m_loc == loc)), own[:, piece_cols:]) + dot(
        hot(hidden_ok & (m_loc != loc)), from_x[:, piece_cols:]
    )
    total, hidden = total.astype(BF16), hidden.astype(BF16)
    for ref, flip_zb, flip_pair in ((keep, 0, 0), (to_1, 1, 0), (to_2, 0, 1), (to_3, 1, 1)):
        ref[:, :piece_cols] = total[flip_zb * count : (flip_zb + 1) * count]
        ref[:, piece_cols:] = hidden[flip_pair * count : (flip_pair + 1) * count]


def expert_kernel(
    own, from_x, from_y, from_xy, down, gate, up, ret_own, ret_y, ret_x, stack
):
    count, piece_cols = from_y.shape
    cap = count // PIECES
    pad = stack.shape[0] // PIECES
    slots = gate.shape[2]
    group, loc, _, _, _ = place()
    source = 2 * group + loc
    m, n = iota((PIECES * pad, count), 0), iota((PIECES * pad, count), 1)
    nq = quotient(n, cap, count)
    n_slot = n - cap * nq
    m_piece, m_slot = m // pad, m % pad
    total = jnp.zeros((PIECES * pad, piece_cols), F32)
    for k, ref in enumerate((own, from_x, from_y, from_xy)):
        match = (m_piece == nq) & (m_slot == (source ^ k) * cap + n_slot)
        total += dot(hot(match), ref[:, :piece_cols])
    slot_rows = total.astype(BF16)
    turned = jnp.zeros((down.shape[1], pad), F32)
    for j in range(PIECES):
        turned += dot_nt(
            down[0, :, j * piece_cols : (j + 1) * piece_cols], slot_rows[j * pad : (j + 1) * pad]
        )
    grad_act = turned.T
    gate_pad = dot(hot(iota((pad, slots), 0) == iota((pad, slots), 1)), gate[0, 0])
    grad_up = (grad_act * gate_pad).astype(BF16)
    for j in range(PIECES):
        part = dot_nt(grad_up, up[0, j * piece_cols : (j + 1) * piece_cols, :])
        stack[j * pad : (j + 1) * pad, :] = part.astype(BF16)
    n, m = iota((count, PIECES * pad), 0), iota((count, PIECES * pad), 1)
    nq = quotient(n, cap, count)
    n_slot = n - cap * nq
    m_piece, m_slot = m // pad, m % pad
    back = []
    for k in range(4):
        match = (m_piece == nq) & (m_slot == (source ^ k) * cap + n_slot)
        back.append(dot(hot(match), stack[...]))
    ret_own[...] = back[0].astype(BF16)
    ret_y[...] = back[2].astype(BF16)
    ret_x[...] = jnp.concatenate([back[1], back[3]], 0).astype(BF16)


def merge_kernel(ret_own, ret_y, from_x, near, far):
    other = from_x[...].astype(F32)
    count = near.shape[0]
    near[...] = (ret_own[...].astype(F32) + other[:count]).astype(BF16)
    far[...] = (ret_y[...].astype(F32) + other[count:]).astype(BF16)


def product_kernel(
    scale, own, from_2, from_3, from_1, swap_own, swap_2, swap_3, swap_1, after, keep, to_xz, to_x,
    to_z, stage
):
    refs = (own, from_2, from_3, from_1, swap_own, swap_2, swap_3, swap_1)
    count = own.shape[0]
    cap = count // PIECES
    slots = 4 * cap
    rows_dev = keep.shape[0]
    piece_cols = keep.shape[1] // 2
    _, loc, zb, _, core = place()
    rows = jnp.concatenate([ref[:, :piece_cols].astype(F32) for ref in refs], 0).astype(BF16)
    m, n = iota((4 * count, count), 0), iota((4 * count, count), 1)
    mq = quotient(m, cap, 4 * count)
    m_slot = m - cap * mq
    m_part, m_loc, m_source, m_has = mq >> 4, (mq >> 3) & 1, (mq >> 1) & 3, mq & 1
    nq = quotient(n, cap, count)
    n_loc, n_row = nq >> 2, n - slots * (nq >> 2)
    ok = (m_has == m_part) & (m_loc == n_loc) & (m_source * cap + m_slot == n_row)
    place_rows = jnp.where(ok, scale, 0.0).astype(BF16)
    spread = [dot(place_rows, ref[:, piece_cols:]) for ref in refs]
    for part in range(2):
        for side in range(2):
            at = (2 * part + side) * count
            hidden = jnp.concatenate([value[at : at + count] for value in spread], 0).T
            pick = [
                jnp.where(
                    core == 0,
                    hidden[2 * k * rows_dev : (2 * k + 1) * rows_dev],
                    hidden[(2 * k + 1) * rows_dev : (2 * k + 2) * rows_dev],
                )
                for k in range(2)
            ]
            product = dot(jnp.concatenate(pick, 0).astype(BF16), rows).astype(BF16)
            cols = slice(part * piece_cols, (part + 1) * piece_cols)
            stage[2 * side, :, cols] = product[:rows_dev]
            stage[2 * side + 1, :, cols] = product[rows_dev:]
    for k, out in enumerate((keep, to_z, to_x, to_xz)):
        out[...] = stage[(2 * loc + zb) ^ k]


def finish_kernel(
    own, from_xz, from_x, from_z, names, near, far, tokens_hbm, down_hbm, tokens_out, down_out, sems
):
    cols = own.shape[1]
    count, piece_cols = near.shape
    cap = count // PIECES
    tokens = tokens_out.shape[1]
    _, loc, zb, _, _ = place()
    copies = []

    def send(source, target):
        copy = pltpu.make_async_copy(source, target, sems.at[len(copies)])
        copy.start()
        copies.append(copy)

    for k, ref in enumerate((own, from_z, from_x, from_xz)):
        start = pl.multiple_of(((2 * loc + zb) ^ k) * cols, cols)
        down_out[k] = ref[...].astype(F32)
        send(down_out.at[k], down_hbm.at[0, :, pl.ds(start, cols)])
    token, lane = iota((tokens, count), 0), iota((tokens, count), 1)
    piece = quotient(lane, cap, count)
    match = [token == names[other : other + 1, :count] for other in range(2)]
    for j in range(PIECES):
        total = dot(hot(match[0] & (piece == j)), near[...]) + dot(
            hot(match[1] & (piece == j)), far[...]
        )
        tokens_out[j] = total.astype(BF16)
        send(tokens_out.at[j], tokens_hbm.at[0, :, pl.ds(j * piece_cols, piece_cols)])
    for copy in copies:
        copy.wait()


VM = pl.BlockSpec(memory_space=pltpu.VMEM)
ANY = pl.BlockSpec(memory_space=pl.ANY)


def call(kernel, outs, args, specs=None, outs_specs=None, scratch=(), flops=0, nbytes=0):
    out_shape = tuple(jax.ShapeDtypeStruct(shape, dtype) for shape, dtype in outs)
    result = pl.pallas_call(
        kernel,
        out_shape=out_shape,
        in_specs=specs or [VM] * len(args),
        out_specs=tuple(outs_specs or [VM] * len(outs)),
        scratch_shapes=list(scratch),
        compiler_params=pltpu.CompilerParams(vmem_limit_bytes=16 * 1024 * 1024),
        cost_estimate=pl.CostEstimate(flops=flops, bytes_accessed=nbytes, transcendentals=0),
    )(*args)
    return result


def hbm(value):
    return pltpu.with_memory_space_constraint(value, pltpu.HBM)


def swap(value, group_flip=0, loc_flip=0, dp_flip=0):
    sizes = [lax.axis_size(axis) for axis in AXES]
    pairs = []
    for g in range(sizes[0]):
        for l in range(sizes[1]):
            for d in range(sizes[2]):
                here = (g * sizes[1] + l) * sizes[2] + d
                there = ((g ^ group_flip) * sizes[1] + (l ^ loc_flip)) * sizes[2] + (d ^ dp_flip)
                pairs.append((here, there))
    return lax.ppermute(value, AXES, pairs)


def local_messages(
    out_grad, slot_token, slot_count, slot_weight, up_weight, down_weight, hidden_saved, gate_saved
):
    model = out_grad.shape[2]
    tokens = out_grad.shape[1]
    cap = slot_token.shape[3]
    hidden_dev = hidden_saved.shape[3]
    replicas = lax.axis_size("dp")
    piece_cols, half, count = model // PIECES, hidden_dev // 2, PIECES * cap
    rows_dev = hidden_dev // replicas
    inputs = (slot_token, slot_count, slot_weight, out_grad, hidden_saved)
    spaces = (pltpu.SMEM, pltpu.SMEM, pltpu.VMEM, pltpu.VMEM, pltpu.VMEM)
    near, far, names = call(
        select_kernel,
        [
            ((count, piece_cols + half), BF16),
            ((count, piece_cols), BF16),
            ((8, 128), jnp.int32),
        ],
        [hbm(x) for x in inputs],
        [ANY] * 5,
        scratch=[space(x.shape, x.dtype) for space, x in zip(spaces, inputs)]
        + [pltpu.SemaphoreType.DMA((5,))],
        nbytes=tokens * model * 2,
    )
    from_xy = swap(far, group_flip=1, loc_flip=1)
    from_y = swap(far, group_flip=1)
    from_x = swap(near, loc_flip=1)
    arrived = (near, from_x, from_y, from_xy)
    held = (down_weight, up_weight, gate_saved)
    down, up, gate = call(
        load_kernel,
        [(x.shape, x.dtype) for x in held],
        [hbm(x) for x in held] + [far],
        [ANY] * 4,
        scratch=[pltpu.SemaphoreType.DMA((3,))],
        nbytes=8 * model * hidden_dev,
    )
    message = ((count, piece_cols + half), BF16)
    mine, to_1, to_2, to_3 = call(
        spread_kernel, [message] * 4, arrived + (gate,), [VM] * 4 + [ANY], nbytes=count * model
    )
    from_2 = swap(to_2, dp_flip=4)
    from_3 = swap(to_3, dp_flip=6)
    from_1 = swap(to_1, dp_flip=2)
    pad = -(-4 * cap // 16) * 16
    part = ((count, piece_cols), BF16)
    ret_own, ret_y, ret_x = call(
        expert_kernel,
        [part, part, ((2 * count, piece_cols), BF16)],
        arrived + (down, gate, up),
        scratch=[pltpu.VMEM((PIECES * pad, piece_cols), BF16)],
        flops=4 * pad * model * hidden_dev,
        nbytes=4 * model * hidden_dev,
    )
    back_x = swap(ret_x, loc_flip=1)
    near_sum, far_sum = call(merge_kernel, [part] * 2, (ret_own, ret_y, back_x), nbytes=1 << 18)
    back_y = swap(far_sum, group_flip=1)
    parts = (mine, from_2, from_3, from_1)
    swapped = tuple(swap(x, dp_flip=1) for x in parts)
    block = ((rows_dev, 2 * piece_cols), BF16)
    own, to_xz, to_x, to_z = call(
        functools.partial(product_kernel, 1.0 / replicas),
        [block] * 4,
        parts + swapped + (ret_own,),
        [VM] * 8 + [ANY],
        scratch=[pltpu.VMEM((4, rows_dev, 2 * piece_cols), BF16)],
        nbytes=1 << 20,
    )
    got_xz = swap(to_xz, loc_flip=1, dp_flip=2)
    got_z = swap(to_z, dp_flip=2)
    got_x = swap(to_x, loc_flip=1)
    input_grad, down_grad = call(
        finish_kernel,
        [((1, tokens, model), BF16), ((1, rows_dev, model), F32)],
        (own, got_xz, got_x, got_z, names, near_sum, back_y),
        outs_specs=[ANY] * 2,
        scratch=[
            pltpu.VMEM((PIECES, tokens, piece_cols), BF16),
            pltpu.VMEM((4, rows_dev, 2 * piece_cols), F32),
            pltpu.SemaphoreType.DMA((4 + PIECES,)),
        ],
        nbytes=4 << 20,
    )
    return (input_grad, down_grad)


def local(*args):
    sizes = tuple(lax.axis_size(axis) for axis in AXES)
    model, cap, hidden_dev = args[0].shape[2], args[1].shape[3], args[6].shape[3]
    fits = sizes == (2, 2, 8) and model % (PIECES * 128) == 0
    fits = fits and hidden_dev % 256 == 0 and args[0].shape[1] % 16 == 0 and 4 * cap <= 32
    return (local_messages if fits else local_collectives)(*args)


def solution(mesh):
    return jax.shard_map(
        local,
        mesh=mesh,
        in_specs=(
            P("dp", ("grp", "loc"), None),
            P("dp", ("grp", "loc"), None, None),
            P("dp", ("grp", "loc"), None),
            P("dp", ("grp", "loc"), None, None),
            P("grp", None, "loc"),
            P("grp", "loc", None),
            P("dp", "grp", None, "loc"),
            P("dp", "grp", None, "loc"),
        ),
        out_specs=(P("dp", ("grp", "loc"), None), P("grp", ("loc", "dp"), None)),
        check_vma=False,
    )
```

```python
import functools

import jax
import jax.numpy as jnp
from jax import lax
from jax.experimental import pallas as pl
from jax.experimental.pallas import tpu as pltpu
from jax.sharding import PartitionSpec as P

AXES = ("grp", "loc", "dp")
PIECES = 8
F32 = jnp.float32
BF16 = jnp.bfloat16


def local_collectives(
    out_grad, slot_token, slot_count, slot_weight, up_weight, down_weight, hidden_saved, gate_saved
):
    group_count = lax.axis_size("grp")
    local_count = lax.axis_size("loc")
    replicas = lax.axis_size("dp")
    grad_rows = out_grad[0]
    tok_dev = grad_rows.shape[0]
    model_dim = grad_rows.shape[1]
    tokens = slot_token[0, 0]
    capacity = tokens.shape[1]
    live_mask = jnp.arange(capacity, dtype=jnp.int32)[None, :] < slot_count[0, 0][:, None]
    picked = jnp.take(grad_rows, tokens.reshape(-1), axis=0).reshape(
        group_count, capacity, model_dim
    )
    outgoing = jnp.where(live_mask[:, :, None], picked, jnp.zeros((), jnp.bfloat16))
    weights = slot_weight[0, 0]
    arrived, arrived_weights = (
        lax.all_to_all(outgoing, "grp", split_axis=0, concat_axis=0, tiled=True),
        lax.all_to_all(weights, "grp", split_axis=0, concat_axis=0, tiled=True),
    )
    rows_all, weights_all = (
        lax.all_gather(arrived[:, None], "loc", axis=1, tiled=True),
        lax.all_gather(arrived_weights[:, None], "loc", axis=1, tiled=True),
    )
    slot_total = group_count * local_count * capacity
    slot_rows = rows_all.reshape(slot_total, model_dim)
    slot_scale = weights_all.reshape(slot_total).astype(jnp.float32)[:, None]
    hidden = hidden_saved[0, 0]
    gate_act = gate_saved[0, 0]
    w_down = down_weight[0]
    w_up = up_weight[0]
    grad_act = lax.dot_general(
        slot_rows, w_down, (((1,), (1,)), ((), ())), preferred_element_type=jnp.float32
    )
    grad_up = (slot_scale * grad_act * gate_act.astype(jnp.float32)).astype(jnp.bfloat16)
    partial_value = lax.dot_general(
        grad_up, w_up, (((1,), (1,)), ((), ())), preferred_element_type=jnp.float32
    )
    partial_value = partial_value.astype(jnp.bfloat16)
    weighted = (slot_scale * hidden.astype(jnp.float32)).astype(jnp.bfloat16)
    product = lax.dot_general(
        weighted, slot_rows, (((0,), (0,)), ((), ())), preferred_element_type=jnp.float32
    )
    rounded = lax.optimization_barrier(product.astype(jnp.bfloat16))
    summed = lax.psum_scatter(
        rounded.astype(jnp.float32).astype(jnp.bfloat16), "dp", scatter_dimension=0, tiled=True
    ).astype(jnp.float32)
    down_grad = (summed / replicas)[None]
    term_rows = lax.optimization_barrier(partial_value).astype(jnp.float32)
    term_rows = term_rows.reshape(group_count, local_count, capacity, model_dim)
    summed_rows = lax.psum_scatter(
        term_rows.astype(jnp.bfloat16), "loc", scatter_dimension=1, tiled=True
    )
    returned = lax.all_to_all(summed_rows, "grp", split_axis=0, concat_axis=0, tiled=True)
    contribs = returned.reshape(group_count * capacity, model_dim)
    matches = jnp.arange(tok_dev, dtype=jnp.int32)[:, None] == tokens.reshape(-1)[None, :]
    onehot = (matches & live_mask.reshape(-1)[None, :]).astype(jnp.bfloat16)
    input_grad = jnp.dot(onehot, contribs, preferred_element_type=jnp.float32).astype(jnp.bfloat16)[
        None
    ]
    return (input_grad, down_grad)


def iota(shape, dim):
    return lax.broadcasted_iota(jnp.int32, shape, dim)


def quotient(value, cap, most):
    shift = 16
    factor = (1 << shift) // cap + 1
    assert all((v * factor) >> shift == v // cap for v in range(most))
    return lax.shift_right_logical(value * factor, shift)


def dot(a, b):
    return jnp.dot(a, b, preferred_element_type=F32)


def dot_nt(a, b):
    return lax.dot_general(a, b, (((1,), (1,)), ((), ())), preferred_element_type=F32)


def hot(condition):
    return jnp.where(condition, 1.0, 0.0).astype(BF16)


def place():
    group, loc, dp = (lax.axis_index(axis) for axis in AXES)
    z = dp // 2
    return group, loc, z % 2, z // 2, dp % 2


def select_kernel(
    tok_hbm, cnt_hbm, weight_hbm, rows_hbm, hidden_hbm, near, far, names, tok, cnt, weight, rows,
    hidden, sems
):
    pairs = (
        (tok_hbm, tok), (cnt_hbm, cnt), (weight_hbm, weight), (rows_hbm, rows), (hidden_hbm, hidden)
    )
    copies = [pltpu.make_async_copy(a, b, sems.at[i]) for i, (a, b) in enumerate(pairs)]
    for copy in copies:
        copy.start()
    cap = tok.shape[3]
    group, _, _, _, _ = place()
    tokens, model = rows.shape[1], rows.shape[2]
    piece_cols = model // PIECES
    count = PIECES * cap
    row, token = iota((count, tokens), 0), iota((count, tokens), 1)
    piece = quotient(row, cap, count)
    slot = row - cap * piece
    lane = iota(names.shape, 1)
    lane_group = quotient(lane, cap, names.shape[1])
    lane_slot = lane - cap * lane_group
    for copy in copies[:3]:
        copy.wait()
    scale = weight[0, 0].astype(F32)
    named = jnp.full(names.shape, -1, jnp.int32)
    values = []
    for other in range(2):
        expert = jnp.where(group == other, 0, 1)
        live = cnt[0, 0, expert]
        value = jnp.zeros((count, tokens), F32)
        for s in range(cap):
            name = jnp.where(s < live, tok[0, 0, expert, s], -1)
            factor = jnp.where(
                expert == 0, scale[0:1, s : s + 1], scale[1:2, s : s + 1]
            )
            value = jnp.where((slot == s) & (token == name), factor, value)
            here = (lane_group // PIECES == other) & (lane_slot == s)
            named = jnp.where(here, name, named)
        values.append(value)
    names[...] = named
    for copy in copies[3:]:
        copy.wait()
    value = jnp.concatenate(values, 0)
    piece = jnp.concatenate([piece, piece], 0)
    total = jnp.zeros((2 * count, piece_cols), F32)
    for j in range(PIECES):
        chosen = jnp.where(piece == j, value, 0.0).astype(BF16)
        total += dot(chosen, rows[0, :, j * piece_cols : (j + 1) * piece_cols])
    near[:, :piece_cols] = total[:count].astype(BF16)
    far[:, :piece_cols] = total[count:].astype(BF16)
    half = hidden.shape[3] // 2
    slots = hidden.shape[2]
    r, c = iota((count, slots), 0), iota((count, slots), 1)
    folded = dot(hot(r == c), hidden[0, 0, :, :half]) + dot(
        hot(r == c + slots), hidden[0, 0, :, half:]
    )
    near[:, piece_cols:] = folded.astype(BF16)
    far[:, piece_cols:] = folded.astype(BF16)


def load_kernel(down_hbm, up_hbm, gate_hbm, after, down, up, gate, sems):
    pairs = ((down_hbm, down), (up_hbm, up), (gate_hbm, gate))
    copies = [pltpu.make_async_copy(a, b, sems.at[i]) for i, (a, b) in enumerate(pairs)]
    for copy in copies:
        copy.start()
    for copy in copies:
        copy.wait()


def spread_kernel(piece_cols, own, from_x, from_y, from_xy, after, keep, to_1, to_2, to_3):
    count = from_y.shape[0]
    cap = count // PIECES
    slots = 4 * cap
    group, loc, zb, pair, _ = place()
    source = 2 * group + loc
    m, n = iota((2 * count, count), 0), iota((2 * count, count), 1)
    mq, nq = quotient(m, cap, 2 * count), quotient(n, cap, count)
    m_slot, n_slot = m - cap * mq, n - cap * nq
    m_flip, m_source, m_part = mq >> 3, (mq >> 1) & 3, mq & 1
    wanted = 4 * loc + 2 * (zb ^ m_flip) + m_part
    rows_ok = (m_slot == n_slot) & (nq == wanted)
    total = jnp.zeros((2 * count, piece_cols), F32)
    for k, ref in enumerate((own, from_x, from_y, from_xy)):
        total += dot(hot(rows_ok & (m_source == (source ^ k))), ref[:, :piece_cols])
    m_loc, m_row = (mq >> 2) & 1, m - slots * (mq >> 2)
    n_half, n_row = nq >> 2, n - slots * (nq >> 2)
    hidden_ok = (m_row == n_row) & (n_half == (pair ^ m_flip))
    hidden = dot(hot(hidden_ok & (m_loc == loc)), own[:, piece_cols:]) + dot(
        hot(hidden_ok & (m_loc != loc)), from_x[:, piece_cols:]
    )
    total, hidden = total.astype(BF16), hidden.astype(BF16)
    for ref, flip_zb, flip_pair in ((keep, 0, 0), (to_1, 1, 0), (to_2, 0, 1), (to_3, 1, 1)):
        ref[:, :piece_cols] = total[flip_zb * count : (flip_zb + 1) * count]
        ref[:, piece_cols:] = hidden[flip_pair * count : (flip_pair + 1) * count]


def expert_kernel(
    own, from_x, from_y, from_xy, down, gate, up, ret_own, ret_y, ret_x, stack
):
    count, piece_cols = ret_y.shape
    cap = count // PIECES
    pad = stack.shape[0] // PIECES
    slots = gate.shape[2]
    group, loc, _, _, _ = place()
    source = 2 * group + loc
    m, n = iota((PIECES * pad, count), 0), iota((PIECES * pad, count), 1)
    nq = quotient(n, cap, count)
    n_slot = n - cap * nq
    m_piece, m_slot = m // pad, m % pad
    total = jnp.zeros((PIECES * pad, piece_cols), F32)
    for k, ref in enumerate((own, from_x, from_y, from_xy)):
        match = (m_piece == nq) & (m_slot == (source ^ k) * cap + n_slot)
        total += dot(hot(match), ref[:, :piece_cols])
    slot_rows = total.astype(BF16)
    turned = jnp.zeros((down.shape[1], pad), F32)
    for j in range(PIECES):
        turned += dot_nt(
            down[0, :, j * piece_cols : (j + 1) * piece_cols], slot_rows[j * pad : (j + 1) * pad]
        )
    grad_act = turned.T
    gate_pad = dot(hot(iota((pad, slots), 0) == iota((pad, slots), 1)), gate[0, 0])
    grad_up = (grad_act * gate_pad).astype(BF16)
    for j in range(PIECES):
        part = dot_nt(grad_up, up[0, j * piece_cols : (j + 1) * piece_cols, :])
        stack[j * pad : (j + 1) * pad, :] = part.astype(BF16)
    n, m = iota((4 * count, PIECES * pad), 0), iota((4 * count, PIECES * pad), 1)
    nq = quotient(n, cap, 4 * count)
    n_slot = n - cap * nq
    m_piece, m_slot = m // pad, m % pad
    back_row = jnp.where(nq < 2 * PIECES, (nq >> 3) * 2, ((nq >> 3) - 2) * 2 + 1)
    match = (m_piece == nq % PIECES) & (m_slot == (source ^ back_row) * cap + n_slot)
    back = dot(hot(match), stack[...])
    ret_own[...] = back[:count].astype(BF16)
    ret_y[...] = back[count : 2 * count].astype(BF16)
    ret_x[...] = back[2 * count :].astype(BF16)


def merge_kernel(ret_own, ret_y, from_x, near, far):
    other = from_x[...].astype(F32)
    count = near.shape[0]
    near[...] = (ret_own[...].astype(F32) + other[:count]).astype(BF16)
    far[...] = (ret_y[...].astype(F32) + other[count:]).astype(BF16)


def product_kernel(
    scale, own, from_2, from_3, from_1, swap_own, swap_2, swap_3, swap_1, after, keep, to_xz, to_x,
    to_z, stage
):
    refs = (own, from_2, from_3, from_1, swap_own, swap_2, swap_3, swap_1)
    count = own.shape[0]
    cap = count // PIECES
    slots = 4 * cap
    rows_dev = keep.shape[0]
    piece_cols = keep.shape[1] // 2
    _, loc, zb, _, core = place()
    rows = jnp.concatenate([ref[:, :piece_cols].astype(F32) for ref in refs], 0).astype(BF16)
    m, n = iota((4 * count, count), 0), iota((4 * count, count), 1)
    mq = quotient(m, cap, 4 * count)
    m_slot = m - cap * mq
    m_part, m_loc, m_source, m_has = mq >> 4, (mq >> 3) & 1, (mq >> 1) & 3, mq & 1
    nq = quotient(n, cap, count)
    n_loc, n_row = nq >> 2, n - slots * (nq >> 2)
    ok = (m_has == m_part) & (m_loc == n_loc) & (m_source * cap + m_slot == n_row)
    place_rows = jnp.where(ok, scale, 0.0).astype(BF16)
    spread = [dot(place_rows, ref[:, piece_cols:]) for ref in refs]
    picks = []
    for block in range(4):
        at = block * count
        hidden = jnp.concatenate([value[at : at + count] for value in spread], 0).T
        for k in range(2):
            first = hidden[2 * k * rows_dev : (2 * k + 1) * rows_dev]
            second = hidden[(2 * k + 1) * rows_dev : (2 * k + 2) * rows_dev]
            picks.append(jnp.where(core == 0, first, second).astype(BF16))
    product = dot(jnp.concatenate(picks, 0), rows).astype(BF16)
    for part in range(2):
        cols = slice(part * piece_cols, (part + 1) * piece_cols)
        for k in range(4):
            at = (4 * part + k) * rows_dev
            stage[k, :, cols] = product[at : at + rows_dev]
    for k, out in enumerate((keep, to_z, to_x, to_xz)):
        out[...] = stage[(2 * loc + zb) ^ k]


def finish_kernel(
    own, from_xz, from_x, from_z, names, near, far, tokens_hbm, down_hbm, tokens_out, down_out, sems
):
    cols = own.shape[1]
    count, piece_cols = near.shape
    cap = count // PIECES
    tokens = tokens_out.shape[1]
    _, loc, zb, _, _ = place()
    copies = []

    def send(source, target):
        copy = pltpu.make_async_copy(source, target, sems.at[len(copies)])
        copy.start()
        copies.append(copy)

    for k, ref in enumerate((own, from_z, from_x, from_xz)):
        start = pl.multiple_of(((2 * loc + zb) ^ k) * cols, cols)
        down_out[k] = ref[...].astype(F32)
        send(down_out.at[k], down_hbm.at[0, :, pl.ds(start, cols)])
    both = jnp.concatenate([near[...].astype(F32), far[...].astype(F32)], 0).astype(BF16)
    token, lane = iota((tokens, 2 * count), 0), iota((tokens, 2 * count), 1)
    piece = quotient(lane, cap, 2 * count) % PIECES
    match = token == names[:1, : 2 * count]
    for j in range(PIECES):
        tokens_out[j] = dot(hot(match & (piece == j)), both).astype(BF16)
        send(tokens_out.at[j], tokens_hbm.at[0, :, pl.ds(j * piece_cols, piece_cols)])
    for copy in copies:
        copy.wait()


VM = pl.BlockSpec(memory_space=pltpu.VMEM)
ANY = pl.BlockSpec(memory_space=pl.ANY)


def call(kernel, outs, args, specs=None, outs_specs=None, scratch=(), flops=0, nbytes=0):
    out_shape = tuple(jax.ShapeDtypeStruct(shape, dtype) for shape, dtype in outs)
    result = pl.pallas_call(
        kernel,
        out_shape=out_shape,
        in_specs=specs or [VM] * len(args),
        out_specs=tuple(outs_specs or [VM] * len(outs)),
        scratch_shapes=list(scratch),
        compiler_params=pltpu.CompilerParams(vmem_limit_bytes=16 * 1024 * 1024),
        cost_estimate=pl.CostEstimate(flops=flops, bytes_accessed=nbytes, transcendentals=0),
    )(*args)
    return result


def hbm(value):
    return pltpu.with_memory_space_constraint(value, pltpu.HBM)


def swap(value, group_flip=0, loc_flip=0, dp_flip=0):
    sizes = [lax.axis_size(axis) for axis in AXES]
    pairs = []
    for g in range(sizes[0]):
        for l in range(sizes[1]):
            for d in range(sizes[2]):
                here = (g * sizes[1] + l) * sizes[2] + d
                there = ((g ^ group_flip) * sizes[1] + (l ^ loc_flip)) * sizes[2] + (d ^ dp_flip)
                pairs.append((here, there))
    return lax.ppermute(value, AXES, pairs)


def local_messages(
    out_grad, slot_token, slot_count, slot_weight, up_weight, down_weight, hidden_saved, gate_saved
):
    model = out_grad.shape[2]
    tokens = out_grad.shape[1]
    cap = slot_token.shape[3]
    hidden_dev = hidden_saved.shape[3]
    replicas = lax.axis_size("dp")
    piece_cols, half, count = model // PIECES, hidden_dev // 2, PIECES * cap
    rows_dev = hidden_dev // replicas
    inputs = (slot_token, slot_count, slot_weight, out_grad, hidden_saved)
    spaces = (pltpu.SMEM, pltpu.SMEM, pltpu.VMEM, pltpu.VMEM, pltpu.VMEM)
    near, far, names = call(
        select_kernel,
        [
            ((count, piece_cols + half), BF16),
            ((count, piece_cols + half), BF16),
            ((8, 128), jnp.int32),
        ],
        [hbm(x) for x in inputs],
        [ANY] * 5,
        scratch=[space(x.shape, x.dtype) for space, x in zip(spaces, inputs)]
        + [pltpu.SemaphoreType.DMA((5,))],
        nbytes=tokens * model * 2,
    )
    from_xy = swap(far, group_flip=1, loc_flip=1)
    from_y = swap(far, group_flip=1)
    from_x = swap(near, loc_flip=1)
    arrived = (near, from_x, from_y, from_xy)
    held = (down_weight, up_weight, gate_saved)
    down, up, gate = call(
        load_kernel,
        [(x.shape, x.dtype) for x in held],
        [hbm(x) for x in held] + [near],
        [ANY] * 4,
        scratch=[pltpu.SemaphoreType.DMA((3,))],
        nbytes=8 * model * hidden_dev,
    )
    message = ((count, piece_cols + half), BF16)
    mine, to_1, to_2, to_3 = call(
        functools.partial(spread_kernel, piece_cols), [message] * 4, arrived + (gate,), [VM] * 4 + [ANY], nbytes=count * model
    )
    from_2 = swap(to_2, dp_flip=4)
    from_3 = swap(to_3, dp_flip=6)
    from_1 = swap(to_1, dp_flip=2)
    pad = -(-4 * cap // 16) * 16
    part = ((count, piece_cols), BF16)
    ret_own, ret_y, ret_x = call(
        expert_kernel,
        [part, part, ((2 * count, piece_cols), BF16)],
        arrived + (down, gate, up),
        scratch=[pltpu.VMEM((PIECES * pad, piece_cols), BF16)],
        flops=4 * pad * model * hidden_dev,
        nbytes=4 * model * hidden_dev,
    )
    back_x = swap(ret_x, loc_flip=1)
    near_sum, far_sum = call(merge_kernel, [part] * 2, (ret_own, ret_y, back_x), nbytes=1 << 18)
    back_y = swap(far_sum, group_flip=1)
    parts = (mine, from_2, from_3, from_1)
    swapped = tuple(swap(x, dp_flip=1) for x in parts)
    block = ((rows_dev, 2 * piece_cols), BF16)
    own, to_xz, to_x, to_z = call(
        functools.partial(product_kernel, 1.0 / replicas),
        [block] * 4,
        parts + swapped + (ret_own,),
        [VM] * 8 + [ANY],
        scratch=[pltpu.VMEM((4, rows_dev, 2 * piece_cols), BF16)],
        nbytes=1 << 20,
    )
    got_xz = swap(to_xz, loc_flip=1, dp_flip=2)
    got_z = swap(to_z, dp_flip=2)
    got_x = swap(to_x, loc_flip=1)
    input_grad, down_grad = call(
        finish_kernel,
        [((1, tokens, model), BF16), ((1, rows_dev, model), F32)],
        (own, got_xz, got_x, got_z, names, near_sum, back_y),
        outs_specs=[ANY] * 2,
        scratch=[
            pltpu.VMEM((PIECES, tokens, piece_cols), BF16),
            pltpu.VMEM((4, rows_dev, 2 * piece_cols), F32),
            pltpu.SemaphoreType.DMA((4 + PIECES,)),
        ],
        nbytes=4 << 20,
    )
    return (input_grad, down_grad)


def local(*args):
    sizes = tuple(lax.axis_size(axis) for axis in AXES)
    model, cap, hidden_dev = args[0].shape[2], args[1].shape[3], args[6].shape[3]
    fits = sizes == (2, 2, 8) and model % (PIECES * 128) == 0
    fits = fits and hidden_dev % 256 == 0 and args[0].shape[1] % 16 == 0 and 4 * cap <= 32
    return (local_messages if fits else local_collectives)(*args)


def solution(mesh):
    return jax.shard_map(
        local,
        mesh=mesh,
        in_specs=(
            P("dp", ("grp", "loc"), None),
            P("dp", ("grp", "loc"), None, None),
            P("dp", ("grp", "loc"), None),
            P("dp", ("grp", "loc"), None, None),
            P("grp", None, "loc"),
            P("grp", "loc", None),
            P("dp", "grp", None, "loc"),
            P("dp", "grp", None, "loc"),
        ),
        out_specs=(P("dp", ("grp", "loc"), None), P("grp", ("loc", "dp"), None)),
        check_vma=False,
    )
```

```python
import functools

import jax
import jax.numpy as jnp
from jax import lax
from jax.experimental import pallas as pl
from jax.experimental.pallas import tpu as pltpu
from jax.sharding import PartitionSpec as P

AXES = ("grp", "loc", "dp")
PIECES = 8
F32 = jnp.float32
BF16 = jnp.bfloat16


def local_collectives(
    out_grad, slot_token, slot_count, slot_weight, up_weight, down_weight, hidden_saved, gate_saved
):
    group_count = lax.axis_size("grp")
    local_count = lax.axis_size("loc")
    replicas = lax.axis_size("dp")
    grad_rows = out_grad[0]
    tok_dev = grad_rows.shape[0]
    model_dim = grad_rows.shape[1]
    tokens = slot_token[0, 0]
    capacity = tokens.shape[1]
    live_mask = jnp.arange(capacity, dtype=jnp.int32)[None, :] < slot_count[0, 0][:, None]
    picked = jnp.take(grad_rows, tokens.reshape(-1), axis=0).reshape(
        group_count, capacity, model_dim
    )
    outgoing = jnp.where(live_mask[:, :, None], picked, jnp.zeros((), jnp.bfloat16))
    weights = slot_weight[0, 0]
    arrived, arrived_weights = (
        lax.all_to_all(outgoing, "grp", split_axis=0, concat_axis=0, tiled=True),
        lax.all_to_all(weights, "grp", split_axis=0, concat_axis=0, tiled=True),
    )
    rows_all, weights_all = (
        lax.all_gather(arrived[:, None], "loc", axis=1, tiled=True),
        lax.all_gather(arrived_weights[:, None], "loc", axis=1, tiled=True),
    )
    slot_total = group_count * local_count * capacity
    slot_rows = rows_all.reshape(slot_total, model_dim)
    slot_scale = weights_all.reshape(slot_total).astype(jnp.float32)[:, None]
    hidden = hidden_saved[0, 0]
    gate_act = gate_saved[0, 0]
    w_down = down_weight[0]
    w_up = up_weight[0]
    grad_act = lax.dot_general(
        slot_rows, w_down, (((1,), (1,)), ((), ())), preferred_element_type=jnp.float32
    )
    grad_up = (slot_scale * grad_act * gate_act.astype(jnp.float32)).astype(jnp.bfloat16)
    partial_value = lax.dot_general(
        grad_up, w_up, (((1,), (1,)), ((), ())), preferred_element_type=jnp.float32
    )
    partial_value = partial_value.astype(jnp.bfloat16)
    weighted = (slot_scale * hidden.astype(jnp.float32)).astype(jnp.bfloat16)
    product = lax.dot_general(
        weighted, slot_rows, (((0,), (0,)), ((), ())), preferred_element_type=jnp.float32
    )
    rounded = lax.optimization_barrier(product.astype(jnp.bfloat16))
    summed = lax.psum_scatter(
        rounded.astype(jnp.float32).astype(jnp.bfloat16), "dp", scatter_dimension=0, tiled=True
    ).astype(jnp.float32)
    down_grad = (summed / replicas)[None]
    term_rows = lax.optimization_barrier(partial_value).astype(jnp.float32)
    term_rows = term_rows.reshape(group_count, local_count, capacity, model_dim)
    summed_rows = lax.psum_scatter(
        term_rows.astype(jnp.bfloat16), "loc", scatter_dimension=1, tiled=True
    )
    returned = lax.all_to_all(summed_rows, "grp", split_axis=0, concat_axis=0, tiled=True)
    contribs = returned.reshape(group_count * capacity, model_dim)
    matches = jnp.arange(tok_dev, dtype=jnp.int32)[:, None] == tokens.reshape(-1)[None, :]
    onehot = (matches & live_mask.reshape(-1)[None, :]).astype(jnp.bfloat16)
    input_grad = jnp.dot(onehot, contribs, preferred_element_type=jnp.float32).astype(jnp.bfloat16)[
        None
    ]
    return (input_grad, down_grad)


def iota(shape, dim):
    return lax.broadcasted_iota(jnp.int32, shape, dim)


def quotient(value, cap, most):
    shift = 16
    factor = (1 << shift) // cap + 1
    assert all((v * factor) >> shift == v // cap for v in range(most))
    return lax.shift_right_logical(value * factor, shift)


def dot(a, b):
    return jnp.dot(a, b, preferred_element_type=F32)


def dot_nt(a, b):
    return lax.dot_general(a, b, (((1,), (1,)), ((), ())), preferred_element_type=F32)


def hot(condition):
    return jnp.where(condition, 1.0, 0.0).astype(BF16)


def place():
    group, loc, dp = (lax.axis_index(axis) for axis in AXES)
    z = dp // 2
    return group, loc, z % 2, z // 2, dp % 2


def select_kernel(
    tok_hbm, cnt_hbm, weight_hbm, rows_hbm, hidden_hbm, near, far, names, tok, cnt, weight, rows,
    hidden, sems
):
    pairs = (
        (tok_hbm, tok), (cnt_hbm, cnt), (weight_hbm, weight), (rows_hbm, rows), (hidden_hbm, hidden)
    )
    copies = [pltpu.make_async_copy(a, b, sems.at[i]) for i, (a, b) in enumerate(pairs)]
    for copy in copies:
        copy.start()
    cap = tok.shape[3]
    group, _, _, _, _ = place()
    tokens, model = rows.shape[1], rows.shape[2]
    piece_cols = model // PIECES
    count = PIECES * cap
    row, token = iota((count, tokens), 0), iota((count, tokens), 1)
    piece = quotient(row, cap, count)
    slot = row - cap * piece
    lane = iota(names.shape, 1)
    lane_group = quotient(lane, cap, names.shape[1])
    lane_slot = lane - cap * lane_group
    for copy in copies[:3]:
        copy.wait()
    scale = weight[0, 0].astype(F32)
    named = jnp.full(names.shape, -1, jnp.int32)
    values = []
    for other in range(2):
        expert = jnp.where(group == other, 0, 1)
        live = cnt[0, 0, expert]
        value = jnp.zeros((count, tokens), F32)
        for s in range(cap):
            name = jnp.where(s < live, tok[0, 0, expert, s], -1)
            factor = jnp.where(
                expert == 0, scale[0:1, s : s + 1], scale[1:2, s : s + 1]
            )
            value = jnp.where((slot == s) & (token == name), factor, value)
            here = (lane_group // PIECES == other) & (lane_slot == s)
            named = jnp.where(here, name, named)
        values.append(value)
    names[...] = named
    for copy in copies[3:]:
        copy.wait()
    value = jnp.concatenate(values, 0)
    piece = jnp.concatenate([piece, piece], 0)
    total = jnp.zeros((2 * count, piece_cols), F32)
    for j in range(PIECES):
        chosen = jnp.where(piece == j, value, 0.0).astype(BF16)
        total += dot(chosen, rows[0, :, j * piece_cols : (j + 1) * piece_cols])
    near[:, :piece_cols] = total[:count].astype(BF16)
    far[:, :piece_cols] = total[count:].astype(BF16)
    half = hidden.shape[3] // 2
    slots = hidden.shape[2]
    r, c = iota((count, slots), 0), iota((count, slots), 1)
    folded = dot(hot(r == c), hidden[0, 0, :, :half]) + dot(
        hot(r == c + slots), hidden[0, 0, :, half:]
    )
    near[:, piece_cols:] = folded.astype(BF16)
    far[:, piece_cols:] = folded.astype(BF16)


def load_kernel(down_hbm, up_hbm, gate_hbm, after, down, up, gate, sems):
    pairs = ((down_hbm, down), (up_hbm, up), (gate_hbm, gate))
    copies = [pltpu.make_async_copy(a, b, sems.at[i]) for i, (a, b) in enumerate(pairs)]
    for copy in copies:
        copy.start()
    for copy in copies:
        copy.wait()


def spread_kernel(piece_cols, own, from_x, from_y, from_xy, after, keep, to_1, to_2, to_3):
    count = from_y.shape[0]
    cap = count // PIECES
    slots = 4 * cap
    group, loc, zb, pair, _ = place()
    source = 2 * group + loc
    m, n = iota((2 * count, count), 0), iota((2 * count, count), 1)
    mq, nq = quotient(m, cap, 2 * count), quotient(n, cap, count)
    m_slot, n_slot = m - cap * mq, n - cap * nq
    m_flip, m_source, m_part = mq >> 3, (mq >> 1) & 3, mq & 1
    wanted = 4 * loc + 2 * (zb ^ m_flip) + m_part
    rows_ok = (m_slot == n_slot) & (nq == wanted)
    total = jnp.zeros((2 * count, piece_cols), F32)
    for k, ref in enumerate((own, from_x, from_y, from_xy)):
        total += dot(hot(rows_ok & (m_source == (source ^ k))), ref[:, :piece_cols])
    m_loc, m_row = (mq >> 2) & 1, m - slots * (mq >> 2)
    n_half, n_row = nq >> 2, n - slots * (nq >> 2)
    hidden_ok = (m_row == n_row) & (n_half == (pair ^ m_flip))
    hidden = dot(hot(hidden_ok & (m_loc == loc)), own[:, piece_cols:]) + dot(
        hot(hidden_ok & (m_loc != loc)), from_x[:, piece_cols:]
    )
    total, hidden = total.astype(BF16), hidden.astype(BF16)
    for ref, flip_zb, flip_pair in ((keep, 0, 0), (to_1, 1, 0), (to_2, 0, 1), (to_3, 1, 1)):
        ref[:, :piece_cols] = total[flip_zb * count : (flip_zb + 1) * count]
        ref[:, piece_cols:] = hidden[flip_pair * count : (flip_pair + 1) * count]


def expert_kernel(
    own, from_x, from_y, from_xy, down, gate, up, ret_own, ret_y, ret_x, stack
):
    count, piece_cols = ret_y.shape
    cap = count // PIECES
    pad = stack.shape[0] // PIECES
    slots = gate.shape[2]
    group, loc, _, _, _ = place()
    source = 2 * group + loc
    m, n = iota((PIECES * pad, count), 0), iota((PIECES * pad, count), 1)
    nq = quotient(n, cap, count)
    n_slot = n - cap * nq
    m_piece, m_slot = m // pad, m % pad
    total = jnp.zeros((PIECES * pad, piece_cols), F32)
    for k, ref in enumerate((own, from_x, from_y, from_xy)):
        match = (m_piece == nq) & (m_slot == (source ^ k) * cap + n_slot)
        total += dot(hot(match), ref[:, :piece_cols])
    slot_rows = total.astype(BF16)
    turned = jnp.zeros((down.shape[1], pad), F32)
    for j in range(PIECES):
        turned += dot_nt(
            down[0, :, j * piece_cols : (j + 1) * piece_cols], slot_rows[j * pad : (j + 1) * pad]
        )
    grad_act = turned.T
    gate_pad = dot(hot(iota((pad, slots), 0) == iota((pad, slots), 1)), gate[0, 0])
    grad_up = (grad_act * gate_pad).astype(BF16)
    for j in range(PIECES):
        part = dot_nt(grad_up, up[0, j * piece_cols : (j + 1) * piece_cols, :])
        stack[j * pad : (j + 1) * pad, :] = part.astype(BF16)
    n, m = iota((4 * count, PIECES * pad), 0), iota((4 * count, PIECES * pad), 1)
    nq = quotient(n, cap, 4 * count)
    n_slot = n - cap * nq
    m_piece, m_slot = m // pad, m % pad
    back_row = jnp.where(nq < 2 * PIECES, (nq >> 3) * 2, ((nq >> 3) - 2) * 2 + 1)
    match = (m_piece == nq % PIECES) & (m_slot == (source ^ back_row) * cap + n_slot)
    back = dot(hot(match), stack[...])
    ret_own[...] = back[:count].astype(BF16)
    ret_y[...] = back[count : 2 * count].astype(BF16)
    ret_x[...] = back[2 * count :].astype(BF16)


def merge_kernel(ret_own, ret_y, from_x, near, far):
    other = from_x[...].astype(F32)
    count = near.shape[0]
    near[...] = (ret_own[...].astype(F32) + other[:count]).astype(BF16)
    far[...] = (ret_y[...].astype(F32) + other[count:]).astype(BF16)


def products(scale, refs, rows_dev, core):
    count = refs[0].shape[0]
    cap = count // PIECES
    slots = 4 * cap
    piece_cols = refs[0].shape[1] - 4 * rows_dev
    rows = jnp.concatenate([ref[:, :piece_cols].astype(F32) for ref in refs], 0).astype(BF16)
    m, n = iota((4 * count, count), 0), iota((4 * count, count), 1)
    mq = quotient(m, cap, 4 * count)
    m_slot = m - cap * mq
    m_part, m_loc, m_source, m_has = mq >> 4, (mq >> 3) & 1, (mq >> 1) & 3, mq & 1
    nq = quotient(n, cap, count)
    n_loc, n_row = nq >> 2, n - slots * (nq >> 2)
    ok = (m_has == m_part) & (m_loc == n_loc) & (m_source * cap + m_slot == n_row)
    place_rows = jnp.where(ok, scale, 0.0).astype(BF16)
    spread = [dot(place_rows, ref[:, piece_cols:]) for ref in refs]
    picks = []
    for block in range(4):
        at = block * count
        hidden = jnp.concatenate([value[at : at + count] for value in spread], 0).T
        for k in range(2):
            first = hidden[2 * k * rows_dev : (2 * k + 1) * rows_dev]
            second = hidden[(2 * k + 1) * rows_dev : (2 * k + 2) * rows_dev]
            picks.append(jnp.where(core == 0, first, second).astype(BF16))
    return dot(jnp.concatenate(picks, 0), rows)


def own_kernel(scale, own, from_2, from_3, from_1, after, total):
    _, _, _, _, core = place()
    total[...] = products(scale, (own, from_2, from_3, from_1), total.shape[0] // 8, core)


def product_kernel(scale, mine, own, from_2, from_3, from_1, keep, to_xz, to_x, to_z, stage):
    rows_dev = keep.shape[0]
    piece_cols = keep.shape[1] // 2
    _, loc, zb, _, core = place()
    other = products(scale, (own, from_2, from_3, from_1), rows_dev, core)
    product = (mine[...] + other).astype(BF16)
    for part in range(2):
        cols = slice(part * piece_cols, (part + 1) * piece_cols)
        for k in range(4):
            at = (4 * part + k) * rows_dev
            stage[k, :, cols] = product[at : at + rows_dev]
    for k, out in enumerate((keep, to_z, to_x, to_xz)):
        out[...] = stage[(2 * loc + zb) ^ k]


def tokens_kernel(names, near, far, out_hbm, out, sems):
    count, piece_cols = near.shape
    cap = count // PIECES
    tokens = out.shape[1]
    both = jnp.concatenate([near[...].astype(F32), far[...].astype(F32)], 0).astype(BF16)
    token, lane = iota((tokens, 2 * count), 0), iota((tokens, 2 * count), 1)
    piece = quotient(lane, cap, 2 * count) % PIECES
    match = token == names[:1, : 2 * count]
    copies = []
    for j in range(PIECES):
        out[j] = dot(hot(match & (piece == j)), both).astype(BF16)
        cols = slice(j * piece_cols, (j + 1) * piece_cols)
        copies.append(pltpu.make_async_copy(out.at[j], out_hbm.at[0, :, cols], sems.at[j]))
        copies[-1].start()
    for copy in copies:
        copy.wait()


def join_kernel(own, from_xz, from_x, from_z, out_hbm, out, sems):
    cols = own.shape[1]
    _, loc, zb, _, _ = place()
    copies = []
    for k, ref in enumerate((own, from_z, from_x, from_xz)):
        start = pl.multiple_of(((2 * loc + zb) ^ k) * cols, cols)
        out[k] = ref[...].astype(F32)
        copy = pltpu.make_async_copy(out.at[k], out_hbm.at[0, :, pl.ds(start, cols)], sems.at[k])
        copy.start()
        copies.append(copy)
    for copy in copies:
        copy.wait()


VM = pl.BlockSpec(memory_space=pltpu.VMEM)
ANY = pl.BlockSpec(memory_space=pl.ANY)


def call(kernel, outs, args, specs=None, outs_specs=None, scratch=(), flops=0, nbytes=0):
    out_shape = tuple(jax.ShapeDtypeStruct(shape, dtype) for shape, dtype in outs)
    result = pl.pallas_call(
        kernel,
        out_shape=out_shape,
        in_specs=specs or [VM] * len(args),
        out_specs=tuple(outs_specs or [VM] * len(outs)),
        scratch_shapes=list(scratch),
        compiler_params=pltpu.CompilerParams(vmem_limit_bytes=16 * 1024 * 1024),
        cost_estimate=pl.CostEstimate(flops=flops, bytes_accessed=nbytes, transcendentals=0),
    )(*args)
    return result


def hbm(value):
    return pltpu.with_memory_space_constraint(value, pltpu.HBM)


def swap(value, group_flip=0, loc_flip=0, dp_flip=0):
    sizes = [lax.axis_size(axis) for axis in AXES]
    pairs = []
    for g in range(sizes[0]):
        for l in range(sizes[1]):
            for d in range(sizes[2]):
                here = (g * sizes[1] + l) * sizes[2] + d
                there = ((g ^ group_flip) * sizes[1] + (l ^ loc_flip)) * sizes[2] + (d ^ dp_flip)
                pairs.append((here, there))
    return lax.ppermute(value, AXES, pairs)


def local_messages(
    out_grad, slot_token, slot_count, slot_weight, up_weight, down_weight, hidden_saved, gate_saved
):
    model = out_grad.shape[2]
    tokens = out_grad.shape[1]
    cap = slot_token.shape[3]
    hidden_dev = hidden_saved.shape[3]
    replicas = lax.axis_size("dp")
    piece_cols, half, count = model // PIECES, hidden_dev // 2, PIECES * cap
    rows_dev = hidden_dev // replicas
    inputs = (slot_token, slot_count, slot_weight, out_grad, hidden_saved)
    spaces = (pltpu.SMEM, pltpu.SMEM, pltpu.VMEM, pltpu.VMEM, pltpu.VMEM)
    near, far, names = call(
        select_kernel,
        [
            ((count, piece_cols + half), BF16),
            ((count, piece_cols + half), BF16),
            ((8, 128), jnp.int32),
        ],
        [hbm(x) for x in inputs],
        [ANY] * 5,
        scratch=[space(x.shape, x.dtype) for space, x in zip(spaces, inputs)]
        + [pltpu.SemaphoreType.DMA((5,))],
        nbytes=tokens * model * 2,
    )
    from_xy = swap(far, group_flip=1, loc_flip=1)
    from_y = swap(far, group_flip=1)
    from_x = swap(near, loc_flip=1)
    arrived = (near, from_x, from_y, from_xy)
    held = (down_weight, up_weight, gate_saved)
    down, up, gate = call(
        load_kernel,
        [(x.shape, x.dtype) for x in held],
        [hbm(x) for x in held] + [near],
        [ANY] * 4,
        scratch=[pltpu.SemaphoreType.DMA((3,))],
        nbytes=8 * model * hidden_dev,
    )
    message = ((count, piece_cols + half), BF16)
    mine, to_1, to_2, to_3 = call(
        functools.partial(spread_kernel, piece_cols), [message] * 4, arrived + (gate,), [VM] * 4 + [ANY], nbytes=count * model
    )
    from_2 = swap(to_2, dp_flip=4)
    from_3 = swap(to_3, dp_flip=6)
    from_1 = swap(to_1, dp_flip=2)
    pad = -(-4 * cap // 16) * 16
    part = ((count, piece_cols), BF16)
    ret_own, ret_y, ret_x = call(
        expert_kernel,
        [part, part, ((2 * count, piece_cols), BF16)],
        arrived + (down, gate, up),
        scratch=[pltpu.VMEM((PIECES * pad, piece_cols), BF16)],
        flops=4 * pad * model * hidden_dev,
        nbytes=4 * model * hidden_dev,
    )
    back_x = swap(ret_x, loc_flip=1)
    near_sum, far_sum = call(merge_kernel, [part] * 2, (ret_own, ret_y, back_x), nbytes=1 << 18)
    back_y = swap(far_sum, group_flip=1)
    parts = (mine, from_2, from_3, from_1)
    swapped = tuple(swap(x, dp_flip=1) for x in parts)
    block = ((rows_dev, 2 * piece_cols), BF16)
    (half_sum,) = call(
        functools.partial(own_kernel, 1.0 / replicas),
        [((8 * rows_dev, piece_cols), F32)],
        parts + (ret_own,),
        [VM] * 4 + [ANY],
        nbytes=1 << 20,
    )
    own, to_xz, to_x, to_z = call(
        functools.partial(product_kernel, 1.0 / replicas),
        [block] * 4,
        (half_sum,) + swapped,
        scratch=[pltpu.VMEM((4, rows_dev, 2 * piece_cols), BF16)],
        nbytes=1 << 20,
    )
    got_xz = swap(to_xz, loc_flip=1, dp_flip=2)
    got_z = swap(to_z, dp_flip=2)
    got_x = swap(to_x, loc_flip=1)
    (input_grad,) = call(
        tokens_kernel,
        [((1, tokens, model), BF16)],
        (names, near_sum, back_y),
        outs_specs=[ANY],
        scratch=[
            pltpu.VMEM((PIECES, tokens, piece_cols), BF16),
            pltpu.SemaphoreType.DMA((PIECES,)),
        ],
        nbytes=2 << 20,
    )
    (down_grad,) = call(
        join_kernel,
        [((1, rows_dev, model), F32)],
        (own, got_xz, got_x, got_z),
        outs_specs=[ANY],
        scratch=[
            pltpu.VMEM((4, rows_dev, 2 * piece_cols), F32),
            pltpu.SemaphoreType.DMA((4,)),
        ],
        nbytes=1 << 20,
    )
    return (input_grad, down_grad)


def local(*args):
    sizes = tuple(lax.axis_size(axis) for axis in AXES)
    model, cap, hidden_dev = args[0].shape[2], args[1].shape[3], args[6].shape[3]
    fits = sizes == (2, 2, 8) and model % (PIECES * 128) == 0
    fits = fits and hidden_dev % 256 == 0 and args[0].shape[1] % 16 == 0 and 4 * cap <= 32
    return (local_messages if fits else local_collectives)(*args)


def solution(mesh):
    return jax.shard_map(
        local,
        mesh=mesh,
        in_specs=(
            P("dp", ("grp", "loc"), None),
            P("dp", ("grp", "loc"), None, None),
            P("dp", ("grp", "loc"), None),
            P("dp", ("grp", "loc"), None, None),
            P("grp", None, "loc"),
            P("grp", "loc", None),
            P("dp", "grp", None, "loc"),
            P("dp", "grp", None, "loc"),
        ),
        out_specs=(P("dp", ("grp", "loc"), None), P("grp", ("loc", "dp"), None)),
        check_vma=False,
    )
```

```python
import functools

import jax
import jax.numpy as jnp
from jax import lax
from jax.experimental import pallas as pl
from jax.experimental.pallas import tpu as pltpu
from jax.sharding import PartitionSpec as P

AXES = ("grp", "loc", "dp")
PIECES = 8
F32 = jnp.float32
BF16 = jnp.bfloat16


def local_collectives(
    out_grad, slot_token, slot_count, slot_weight, up_weight, down_weight, hidden_saved, gate_saved
):
    group_count = lax.axis_size("grp")
    local_count = lax.axis_size("loc")
    replicas = lax.axis_size("dp")
    grad_rows = out_grad[0]
    tok_dev = grad_rows.shape[0]
    model_dim = grad_rows.shape[1]
    tokens = slot_token[0, 0]
    capacity = tokens.shape[1]
    live_mask = jnp.arange(capacity, dtype=jnp.int32)[None, :] < slot_count[0, 0][:, None]
    picked = jnp.take(grad_rows, tokens.reshape(-1), axis=0).reshape(
        group_count, capacity, model_dim
    )
    outgoing = jnp.where(live_mask[:, :, None], picked, jnp.zeros((), jnp.bfloat16))
    weights = slot_weight[0, 0]
    arrived, arrived_weights = (
        lax.all_to_all(outgoing, "grp", split_axis=0, concat_axis=0, tiled=True),
        lax.all_to_all(weights, "grp", split_axis=0, concat_axis=0, tiled=True),
    )
    rows_all, weights_all = (
        lax.all_gather(arrived[:, None], "loc", axis=1, tiled=True),
        lax.all_gather(arrived_weights[:, None], "loc", axis=1, tiled=True),
    )
    slot_total = group_count * local_count * capacity
    slot_rows = rows_all.reshape(slot_total, model_dim)
    slot_scale = weights_all.reshape(slot_total).astype(jnp.float32)[:, None]
    hidden = hidden_saved[0, 0]
    gate_act = gate_saved[0, 0]
    w_down = down_weight[0]
    w_up = up_weight[0]
    grad_act = lax.dot_general(
        slot_rows, w_down, (((1,), (1,)), ((), ())), preferred_element_type=jnp.float32
    )
    grad_up = (slot_scale * grad_act * gate_act.astype(jnp.float32)).astype(jnp.bfloat16)
    partial_value = lax.dot_general(
        grad_up, w_up, (((1,), (1,)), ((), ())), preferred_element_type=jnp.float32
    )
    partial_value = partial_value.astype(jnp.bfloat16)
    weighted = (slot_scale * hidden.astype(jnp.float32)).astype(jnp.bfloat16)
    product = lax.dot_general(
        weighted, slot_rows, (((0,), (0,)), ((), ())), preferred_element_type=jnp.float32
    )
    rounded = lax.optimization_barrier(product.astype(jnp.bfloat16))
    summed = lax.psum_scatter(
        rounded.astype(jnp.float32).astype(jnp.bfloat16), "dp", scatter_dimension=0, tiled=True
    ).astype(jnp.float32)
    down_grad = (summed / replicas)[None]
    term_rows = lax.optimization_barrier(partial_value).astype(jnp.float32)
    term_rows = term_rows.reshape(group_count, local_count, capacity, model_dim)
    summed_rows = lax.psum_scatter(
        term_rows.astype(jnp.bfloat16), "loc", scatter_dimension=1, tiled=True
    )
    returned = lax.all_to_all(summed_rows, "grp", split_axis=0, concat_axis=0, tiled=True)
    contribs = returned.reshape(group_count * capacity, model_dim)
    matches = jnp.arange(tok_dev, dtype=jnp.int32)[:, None] == tokens.reshape(-1)[None, :]
    onehot = (matches & live_mask.reshape(-1)[None, :]).astype(jnp.bfloat16)
    input_grad = jnp.dot(onehot, contribs, preferred_element_type=jnp.float32).astype(jnp.bfloat16)[
        None
    ]
    return (input_grad, down_grad)


def iota(shape, dim):
    return lax.broadcasted_iota(jnp.int32, shape, dim)


def quotient(value, cap, most):
    shift = 16
    factor = (1 << shift) // cap + 1
    assert all((v * factor) >> shift == v // cap for v in range(most))
    return lax.shift_right_logical(value * factor, shift)


def dot(a, b):
    return jnp.dot(a, b, preferred_element_type=F32)


def dot_nt(a, b):
    return lax.dot_general(a, b, (((1,), (1,)), ((), ())), preferred_element_type=F32)


def hot(condition):
    return jnp.where(condition, 1.0, 0.0).astype(BF16)


def place():
    group, loc, dp = (lax.axis_index(axis) for axis in AXES)
    z = dp // 2
    return group, loc, z % 2, z // 2, dp % 2


def select_kernel(
    tok_hbm, cnt_hbm, weight_hbm, rows_hbm, hidden_hbm, near, far, names, tok, cnt, weight, rows,
    hidden, sems
):
    pairs = (
        (tok_hbm, tok), (cnt_hbm, cnt), (weight_hbm, weight), (rows_hbm, rows), (hidden_hbm, hidden)
    )
    copies = [pltpu.make_async_copy(a, b, sems.at[i]) for i, (a, b) in enumerate(pairs)]
    for i in (3, 0, 1, 2, 4):
        copies[i].start()
    cap = tok.shape[3]
    group, _, _, _, _ = place()
    tokens, model = rows.shape[1], rows.shape[2]
    piece_cols = model // PIECES
    count = PIECES * cap
    row, token = iota((count, tokens), 0), iota((count, tokens), 1)
    piece = quotient(row, cap, count)
    slot = row - cap * piece
    lane = iota(names.shape, 1)
    lane_group = quotient(lane, cap, names.shape[1])
    lane_slot = lane - cap * lane_group
    for copy in copies[:3]:
        copy.wait()
    scale = weight[0, 0].astype(F32)
    named = jnp.full(names.shape, -1, jnp.int32)
    values = []
    for other in range(2):
        expert = jnp.where(group == other, 0, 1)
        live = cnt[0, 0, expert]
        value = jnp.zeros((count, tokens), F32)
        for s in range(cap):
            name = jnp.where(s < live, tok[0, 0, expert, s], -1)
            factor = jnp.where(
                expert == 0, scale[0:1, s : s + 1], scale[1:2, s : s + 1]
            )
            value = jnp.where((slot == s) & (token == name), factor, value)
            here = (lane_group // PIECES == other) & (lane_slot == s)
            named = jnp.where(here, name, named)
        values.append(value)
    names[...] = named
    for copy in copies[3:]:
        copy.wait()
    value = jnp.concatenate(values, 0)
    piece = jnp.concatenate([piece, piece], 0)
    total = jnp.zeros((2 * count, piece_cols), F32)
    for j in range(PIECES):
        chosen = jnp.where(piece == j, value, 0.0).astype(BF16)
        total += dot(chosen, rows[0, :, j * piece_cols : (j + 1) * piece_cols])
    near[:, :piece_cols] = total[:count].astype(BF16)
    far[:, :piece_cols] = total[count:].astype(BF16)
    half = hidden.shape[3] // 2
    slots = hidden.shape[2]
    r, c = iota((count, slots), 0), iota((count, slots), 1)
    folded = dot(hot(r == c), hidden[0, 0, :, :half]) + dot(
        hot(r == c + slots), hidden[0, 0, :, half:]
    )
    near[:, piece_cols:] = folded.astype(BF16)
    far[:, piece_cols:] = folded.astype(BF16)


def load_kernel(down_hbm, up_hbm, gate_hbm, after, down, up, gate, sems):
    pairs = ((down_hbm, down), (up_hbm, up), (gate_hbm, gate))
    copies = [pltpu.make_async_copy(a, b, sems.at[i]) for i, (a, b) in enumerate(pairs)]
    for copy in copies:
        copy.start()
    for copy in copies:
        copy.wait()


def spread_kernel(piece_cols, own, from_x, from_y, from_xy, after, keep, to_1, to_2, to_3):
    count = from_y.shape[0]
    cap = count // PIECES
    slots = 4 * cap
    group, loc, zb, pair, _ = place()
    source = 2 * group + loc
    m, n = iota((2 * count, count), 0), iota((2 * count, count), 1)
    mq, nq = quotient(m, cap, 2 * count), quotient(n, cap, count)
    m_slot, n_slot = m - cap * mq, n - cap * nq
    m_flip, m_source, m_part = mq >> 3, (mq >> 1) & 3, mq & 1
    wanted = 4 * loc + 2 * (zb ^ m_flip) + m_part
    rows_ok = (m_slot == n_slot) & (nq == wanted)
    total = jnp.zeros((2 * count, piece_cols), F32)
    for k, ref in enumerate((own, from_x, from_y, from_xy)):
        total += dot(hot(rows_ok & (m_source == (source ^ k))), ref[:, :piece_cols])
    m_loc, m_row = (mq >> 2) & 1, m - slots * (mq >> 2)
    n_half, n_row = nq >> 2, n - slots * (nq >> 2)
    hidden_ok = (m_row == n_row) & (n_half == (pair ^ m_flip))
    hidden = dot(hot(hidden_ok & (m_loc == loc)), own[:, piece_cols:]) + dot(
        hot(hidden_ok & (m_loc != loc)), from_x[:, piece_cols:]
    )
    total, hidden = total.astype(BF16), hidden.astype(BF16)
    for ref, flip_zb, flip_pair in ((keep, 0, 0), (to_1, 1, 0), (to_2, 0, 1), (to_3, 1, 1)):
        ref[:, :piece_cols] = total[flip_zb * count : (flip_zb + 1) * count]
        ref[:, piece_cols:] = hidden[flip_pair * count : (flip_pair + 1) * count]


def expert_kernel(
    own, from_x, from_y, from_xy, down, gate, up, ret_own, ret_y, ret_x, stack
):
    count, piece_cols = ret_y.shape
    cap = count // PIECES
    pad = stack.shape[0] // PIECES
    slots = gate.shape[2]
    group, loc, _, _, _ = place()
    source = 2 * group + loc
    m, n = iota((PIECES * pad, count), 0), iota((PIECES * pad, count), 1)
    nq = quotient(n, cap, count)
    n_slot = n - cap * nq
    m_piece, m_slot = m // pad, m % pad
    total = jnp.zeros((PIECES * pad, piece_cols), F32)
    for k, ref in enumerate((own, from_x, from_y, from_xy)):
        match = (m_piece == nq) & (m_slot == (source ^ k) * cap + n_slot)
        total += dot(hot(match), ref[:, :piece_cols])
    slot_rows = total.astype(BF16)
    turned = jnp.zeros((down.shape[1], pad), F32)
    for j in range(PIECES):
        turned += dot_nt(
            down[0, :, j * piece_cols : (j + 1) * piece_cols], slot_rows[j * pad : (j + 1) * pad]
        )
    grad_act = turned.T
    gate_pad = dot(hot(iota((pad, slots), 0) == iota((pad, slots), 1)), gate[0, 0])
    grad_up = (grad_act * gate_pad).astype(BF16)
    for j in range(PIECES):
        part = dot_nt(grad_up, up[0, j * piece_cols : (j + 1) * piece_cols, :])
        stack[j * pad : (j + 1) * pad, :] = part.astype(BF16)
    n, m = iota((4 * count, PIECES * pad), 0), iota((4 * count, PIECES * pad), 1)
    nq = quotient(n, cap, 4 * count)
    n_slot = n - cap * nq
    m_piece, m_slot = m // pad, m % pad
    back_row = jnp.where(nq < 2 * PIECES, (nq >> 3) * 2, ((nq >> 3) - 2) * 2 + 1)
    match = (m_piece == nq % PIECES) & (m_slot == (source ^ back_row) * cap + n_slot)
    back = dot(hot(match), stack[...])
    ret_own[...] = back[:count].astype(BF16)
    ret_y[...] = back[count : 2 * count].astype(BF16)
    ret_x[...] = back[2 * count :].astype(BF16)


def merge_kernel(ret_own, ret_y, from_x, near, far):
    other = from_x[...].astype(F32)
    count = near.shape[0]
    near[...] = (ret_own[...].astype(F32) + other[:count]).astype(BF16)
    far[...] = (ret_y[...].astype(F32) + other[count:]).astype(BF16)


def products(scale, refs, rows_dev, core):
    count = refs[0].shape[0]
    cap = count // PIECES
    slots = 4 * cap
    piece_cols = refs[0].shape[1] - 4 * rows_dev
    rows = jnp.concatenate([ref[:, :piece_cols].astype(F32) for ref in refs], 0).astype(BF16)
    m, n = iota((4 * count, count), 0), iota((4 * count, count), 1)
    mq = quotient(m, cap, 4 * count)
    m_slot = m - cap * mq
    m_part, m_loc, m_source, m_has = mq >> 4, (mq >> 3) & 1, (mq >> 1) & 3, mq & 1
    nq = quotient(n, cap, count)
    n_loc, n_row = nq >> 2, n - slots * (nq >> 2)
    ok = (m_has == m_part) & (m_loc == n_loc) & (m_source * cap + m_slot == n_row)
    place_rows = jnp.where(ok, scale, 0.0).astype(BF16)
    wide = 4 * rows_dev
    every = dot(place_rows, jnp.concatenate([ref[:, piece_cols:] for ref in refs], 1))
    spread = [every[:, k * wide : (k + 1) * wide] for k in range(len(refs))]
    picks = []
    for block in range(4):
        at = block * count
        hidden = jnp.concatenate([value[at : at + count] for value in spread], 0).T
        for k in range(2):
            first = hidden[2 * k * rows_dev : (2 * k + 1) * rows_dev]
            second = hidden[(2 * k + 1) * rows_dev : (2 * k + 2) * rows_dev]
            picks.append(jnp.where(core == 0, first, second).astype(BF16))
    return dot(jnp.concatenate(picks, 0), rows)


def early_kernel(scale, own, from_2, from_3, from_1, swap_own, swap_2, after, total):
    _, _, _, _, core = place()
    refs = (own, from_2, from_3, from_1, swap_own, swap_2)
    total[...] = products(scale, refs, total.shape[0] // 8, core)


def product_kernel(scale, early, swap_3, swap_1, keep, to_xz, to_x, to_z, stage):
    rows_dev = keep.shape[0]
    piece_cols = keep.shape[1] // 2
    _, loc, zb, _, core = place()
    late = products(scale, (swap_3, swap_1), rows_dev, core)
    product = (early[...] + late).astype(BF16)
    for part in range(2):
        cols = slice(part * piece_cols, (part + 1) * piece_cols)
        for k in range(4):
            at = (4 * part + k) * rows_dev
            stage[k, :, cols] = product[at : at + rows_dev]
    for k, out in enumerate((keep, to_z, to_x, to_xz)):
        out[...] = stage[(2 * loc + zb) ^ k]


def tokens_kernel(names, near, far, out):
    count, piece_cols = near.shape
    cap = count // PIECES
    tokens = out.shape[1]
    both = jnp.concatenate([near[...].astype(F32), far[...].astype(F32)], 0).astype(BF16)
    token, lane = iota((tokens, 2 * count), 0), iota((tokens, 2 * count), 1)
    piece = quotient(lane, cap, 2 * count) % PIECES
    match = token == names[:1, : 2 * count]
    for j in range(PIECES):
        total = dot(hot(match & (piece == j)), both).astype(BF16)
        out[0, :, j * piece_cols : (j + 1) * piece_cols] = total


def join_kernel(own, from_xz, from_x, from_z, summed, tokens_hbm, down_hbm, out, sems):
    cols = own.shape[1]
    _, loc, zb, _, _ = place()
    copies = [pltpu.make_async_copy(summed, tokens_hbm, sems.at[4])]
    copies[0].start()
    for k, ref in enumerate((own, from_z, from_x, from_xz)):
        start = pl.multiple_of(((2 * loc + zb) ^ k) * cols, cols)
        out[k] = ref[...].astype(F32)
        copy = pltpu.make_async_copy(out.at[k], down_hbm.at[0, :, pl.ds(start, cols)], sems.at[k])
        copy.start()
        copies.append(copy)
    for copy in copies:
        copy.wait()


VM = pl.BlockSpec(memory_space=pltpu.VMEM)
ANY = pl.BlockSpec(memory_space=pl.ANY)


def call(kernel, outs, args, specs=None, outs_specs=None, scratch=(), flops=0, nbytes=0):
    out_shape = tuple(jax.ShapeDtypeStruct(shape, dtype) for shape, dtype in outs)
    result = pl.pallas_call(
        kernel,
        out_shape=out_shape,
        in_specs=specs or [VM] * len(args),
        out_specs=tuple(outs_specs or [VM] * len(outs)),
        scratch_shapes=list(scratch),
        compiler_params=pltpu.CompilerParams(vmem_limit_bytes=16 * 1024 * 1024),
        cost_estimate=pl.CostEstimate(flops=flops, bytes_accessed=nbytes, transcendentals=0),
    )(*args)
    return result


def hbm(value):
    return pltpu.with_memory_space_constraint(value, pltpu.HBM)


def swap(value, group_flip=0, loc_flip=0, dp_flip=0):
    sizes = [lax.axis_size(axis) for axis in AXES]
    pairs = []
    for g in range(sizes[0]):
        for l in range(sizes[1]):
            for d in range(sizes[2]):
                here = (g * sizes[1] + l) * sizes[2] + d
                there = ((g ^ group_flip) * sizes[1] + (l ^ loc_flip)) * sizes[2] + (d ^ dp_flip)
                pairs.append((here, there))
    return lax.ppermute(value, AXES, pairs)


def local_messages(
    out_grad, slot_token, slot_count, slot_weight, up_weight, down_weight, hidden_saved, gate_saved
):
    model = out_grad.shape[2]
    tokens = out_grad.shape[1]
    cap = slot_token.shape[3]
    hidden_dev = hidden_saved.shape[3]
    replicas = lax.axis_size("dp")
    piece_cols, half, count = model // PIECES, hidden_dev // 2, PIECES * cap
    rows_dev = hidden_dev // replicas
    inputs = (slot_token, slot_count, slot_weight, out_grad, hidden_saved)
    spaces = (pltpu.SMEM, pltpu.SMEM, pltpu.VMEM, pltpu.VMEM, pltpu.VMEM)
    near, far, names = call(
        select_kernel,
        [
            ((count, piece_cols + half), BF16),
            ((count, piece_cols + half), BF16),
            ((8, 128), jnp.int32),
        ],
        [hbm(x) for x in inputs],
        [ANY] * 5,
        scratch=[space(x.shape, x.dtype) for space, x in zip(spaces, inputs)]
        + [pltpu.SemaphoreType.DMA((5,))],
        nbytes=tokens * model * 2,
    )
    from_xy = swap(far, group_flip=1, loc_flip=1)
    from_y = swap(far, group_flip=1)
    from_x = swap(near, loc_flip=1)
    arrived = (near, from_x, from_y, from_xy)
    held = (down_weight, up_weight, gate_saved)
    down, up, gate = call(
        load_kernel,
        [(x.shape, x.dtype) for x in held],
        [hbm(x) for x in held] + [near],
        [ANY] * 4,
        scratch=[pltpu.SemaphoreType.DMA((3,))],
        nbytes=8 * model * hidden_dev,
    )
    message = ((count, piece_cols + half), BF16)
    mine, to_1, to_2, to_3 = call(
        functools.partial(spread_kernel, piece_cols), [message] * 4, arrived + (gate,), [VM] * 4 + [ANY], nbytes=count * model
    )
    from_2 = swap(to_2, dp_flip=4)
    from_3 = swap(to_3, dp_flip=6)
    from_1 = swap(to_1, dp_flip=2)
    pad = -(-4 * cap // 16) * 16
    part = ((count, piece_cols), BF16)
    ret_own, ret_y, ret_x = call(
        expert_kernel,
        [part, part, ((2 * count, piece_cols), BF16)],
        arrived + (down, gate, up),
        scratch=[pltpu.VMEM((PIECES * pad, piece_cols), BF16)],
        flops=4 * pad * model * hidden_dev,
        nbytes=4 * model * hidden_dev,
    )
    back_x = swap(ret_x, loc_flip=1)
    near_sum, far_sum = call(merge_kernel, [part] * 2, (ret_own, ret_y, back_x), nbytes=1 << 18)
    back_y = swap(far_sum, group_flip=1)
    parts = (mine, from_2, from_3, from_1)
    swapped = tuple(swap(x, dp_flip=1) for x in parts)
    block = ((rows_dev, 2 * piece_cols), BF16)
    (early_sum,) = call(
        functools.partial(early_kernel, 1.0 / replicas),
        [((8 * rows_dev, piece_cols), F32)],
        parts + swapped[:2] + (ret_own,),
        [VM] * 6 + [ANY],
        nbytes=1 << 20,
    )
    own, to_xz, to_x, to_z = call(
        functools.partial(product_kernel, 1.0 / replicas),
        [block] * 4,
        (early_sum,) + swapped[2:],
        scratch=[pltpu.VMEM((4, rows_dev, 2 * piece_cols), BF16)],
        nbytes=1 << 20,
    )
    got_xz = swap(to_xz, loc_flip=1, dp_flip=2)
    got_z = swap(to_z, dp_flip=2)
    got_x = swap(to_x, loc_flip=1)
    (summed,) = call(
        tokens_kernel,
        [((1, tokens, model), BF16)],
        (names, near_sum, back_y),
        nbytes=2 << 20,
    )
    input_grad, down_grad = call(
        join_kernel,
        [((1, tokens, model), BF16), ((1, rows_dev, model), F32)],
        (own, got_xz, got_x, got_z, summed),
        outs_specs=[ANY] * 2,
        scratch=[
            pltpu.VMEM((4, rows_dev, 2 * piece_cols), F32),
            pltpu.SemaphoreType.DMA((5,)),
        ],
        nbytes=1 << 20,
    )
    return (input_grad, down_grad)


def local(*args):
    sizes = tuple(lax.axis_size(axis) for axis in AXES)
    model, cap, hidden_dev = args[0].shape[2], args[1].shape[3], args[6].shape[3]
    fits = sizes == (2, 2, 8) and model % (PIECES * 128) == 0
    fits = fits and hidden_dev % 256 == 0 and args[0].shape[1] % 16 == 0 and 4 * cap <= 32
    return (local_messages if fits else local_collectives)(*args)


def solution(mesh):
    return jax.shard_map(
        local,
        mesh=mesh,
        in_specs=(
            P("dp", ("grp", "loc"), None),
            P("dp", ("grp", "loc"), None, None),
            P("dp", ("grp", "loc"), None),
            P("dp", ("grp", "loc"), None, None),
            P("grp", None, "loc"),
            P("grp", "loc", None),
            P("dp", "grp", None, "loc"),
            P("dp", "grp", None, "loc"),
        ),
        out_specs=(P("dp", ("grp", "loc"), None), P("grp", ("loc", "dp"), None)),
        check_vma=False,
    )
```

```python
import functools

import jax
import jax.numpy as jnp
from jax import lax
from jax.experimental import pallas as pl
from jax.experimental.pallas import tpu as pltpu
from jax.sharding import PartitionSpec as P

AXES = ("grp", "loc", "dp")
PIECES = 8
F32 = jnp.float32
BF16 = jnp.bfloat16


def local_collectives(
    out_grad, slot_token, slot_count, slot_weight, up_weight, down_weight, hidden_saved, gate_saved
):
    group_count = lax.axis_size("grp")
    local_count = lax.axis_size("loc")
    replicas = lax.axis_size("dp")
    grad_rows = out_grad[0]
    tok_dev = grad_rows.shape[0]
    model_dim = grad_rows.shape[1]
    tokens = slot_token[0, 0]
    capacity = tokens.shape[1]
    live_mask = jnp.arange(capacity, dtype=jnp.int32)[None, :] < slot_count[0, 0][:, None]
    picked = jnp.take(grad_rows, tokens.reshape(-1), axis=0).reshape(
        group_count, capacity, model_dim
    )
    outgoing = jnp.where(live_mask[:, :, None], picked, jnp.zeros((), jnp.bfloat16))
    weights = slot_weight[0, 0]
    arrived, arrived_weights = (
        lax.all_to_all(outgoing, "grp", split_axis=0, concat_axis=0, tiled=True),
        lax.all_to_all(weights, "grp", split_axis=0, concat_axis=0, tiled=True),
    )
    rows_all, weights_all = (
        lax.all_gather(arrived[:, None], "loc", axis=1, tiled=True),
        lax.all_gather(arrived_weights[:, None], "loc", axis=1, tiled=True),
    )
    slot_total = group_count * local_count * capacity
    slot_rows = rows_all.reshape(slot_total, model_dim)
    slot_scale = weights_all.reshape(slot_total).astype(jnp.float32)[:, None]
    hidden = hidden_saved[0, 0]
    gate_act = gate_saved[0, 0]
    w_down = down_weight[0]
    w_up = up_weight[0]
    grad_act = lax.dot_general(
        slot_rows, w_down, (((1,), (1,)), ((), ())), preferred_element_type=jnp.float32
    )
    grad_up = (slot_scale * grad_act * gate_act.astype(jnp.float32)).astype(jnp.bfloat16)
    partial_value = lax.dot_general(
        grad_up, w_up, (((1,), (1,)), ((), ())), preferred_element_type=jnp.float32
    )
    partial_value = partial_value.astype(jnp.bfloat16)
    weighted = (slot_scale * hidden.astype(jnp.float32)).astype(jnp.bfloat16)
    product = lax.dot_general(
        weighted, slot_rows, (((0,), (0,)), ((), ())), preferred_element_type=jnp.float32
    )
    rounded = lax.optimization_barrier(product.astype(jnp.bfloat16))
    summed = lax.psum_scatter(
        rounded.astype(jnp.float32).astype(jnp.bfloat16), "dp", scatter_dimension=0, tiled=True
    ).astype(jnp.float32)
    down_grad = (summed / replicas)[None]
    term_rows = lax.optimization_barrier(partial_value).astype(jnp.float32)
    term_rows = term_rows.reshape(group_count, local_count, capacity, model_dim)
    summed_rows = lax.psum_scatter(
        term_rows.astype(jnp.bfloat16), "loc", scatter_dimension=1, tiled=True
    )
    returned = lax.all_to_all(summed_rows, "grp", split_axis=0, concat_axis=0, tiled=True)
    contribs = returned.reshape(group_count * capacity, model_dim)
    matches = jnp.arange(tok_dev, dtype=jnp.int32)[:, None] == tokens.reshape(-1)[None, :]
    onehot = (matches & live_mask.reshape(-1)[None, :]).astype(jnp.bfloat16)
    input_grad = jnp.dot(onehot, contribs, preferred_element_type=jnp.float32).astype(jnp.bfloat16)[
        None
    ]
    return (input_grad, down_grad)


def iota(shape, dim):
    return lax.broadcasted_iota(jnp.int32, shape, dim)


def quotient(value, cap, most):
    shift = 16
    factor = (1 << shift) // cap + 1
    assert all((v * factor) >> shift == v // cap for v in range(most))
    return lax.shift_right_logical(value * factor, shift)


def dot(a, b):
    return jnp.dot(a, b, preferred_element_type=F32)


def dot_nt(a, b):
    return lax.dot_general(a, b, (((1,), (1,)), ((), ())), preferred_element_type=F32)


def hot(condition):
    return jnp.where(condition, 1.0, 0.0).astype(BF16)


def place():
    group, loc, dp = (lax.axis_index(axis) for axis in AXES)
    z = dp // 2
    return group, loc, z % 2, z // 2, dp % 2


def select_kernel(
    tok_hbm, cnt_hbm, weight_hbm, rows_hbm, hidden_hbm, near, far, names, tok, cnt, weight, rows,
    hidden, sems
):
    pairs = (
        (tok_hbm, tok), (cnt_hbm, cnt), (weight_hbm, weight), (rows_hbm, rows), (hidden_hbm, hidden)
    )
    copies = [pltpu.make_async_copy(a, b, sems.at[i]) for i, (a, b) in enumerate(pairs)]
    for i in (3, 0, 1, 2, 4):
        copies[i].start()
    cap = tok.shape[3]
    group, _, _, _, _ = place()
    tokens, model = rows.shape[1], rows.shape[2]
    piece_cols = model // PIECES
    count = PIECES * cap
    row, token = iota((count, tokens), 0), iota((count, tokens), 1)
    piece = quotient(row, cap, count)
    slot = row - cap * piece
    lane = iota(names.shape, 1)
    lane_group = quotient(lane, cap, names.shape[1])
    lane_slot = lane - cap * lane_group
    for copy in copies[:3]:
        copy.wait()
    scale = weight[0, 0].astype(F32)
    named = jnp.full(names.shape, -1, jnp.int32)
    values = []
    for other in range(2):
        expert = jnp.where(group == other, 0, 1)
        live = cnt[0, 0, expert]
        value = jnp.zeros((count, tokens), F32)
        for s in range(cap):
            name = jnp.where(s < live, tok[0, 0, expert, s], -1)
            factor = jnp.where(
                expert == 0, scale[0:1, s : s + 1], scale[1:2, s : s + 1]
            )
            value = jnp.where((slot == s) & (token == name), factor, value)
            here = (lane_group // PIECES == other) & (lane_slot == s)
            named = jnp.where(here, name, named)
        values.append(value)
    names[...] = named
    for copy in copies[3:]:
        copy.wait()
    value = jnp.concatenate(values, 0)
    piece = jnp.concatenate([piece, piece], 0)
    total = jnp.zeros((2 * count, piece_cols), F32)
    for j in range(PIECES):
        chosen = jnp.where(piece == j, value, 0.0).astype(BF16)
        total += dot(chosen, rows[0, :, j * piece_cols : (j + 1) * piece_cols])
    near[:, :piece_cols] = total[:count].astype(BF16)
    far[:, :piece_cols] = total[count:].astype(BF16)
    half = hidden.shape[3] // 2
    slots = hidden.shape[2]
    r, c = iota((count, slots), 0), iota((count, slots), 1)
    folded = dot(hot(r == c), hidden[0, 0, :, :half]) + dot(
        hot(r == c + slots), hidden[0, 0, :, half:]
    )
    near[:, piece_cols:] = folded.astype(BF16)
    far[:, piece_cols:] = folded.astype(BF16)


def load_kernel(down_hbm, up_hbm, gate_hbm, after, down, up, gate, sems):
    pairs = ((down_hbm, down), (up_hbm, up), (gate_hbm, gate))
    copies = [pltpu.make_async_copy(a, b, sems.at[i]) for i, (a, b) in enumerate(pairs)]
    for copy in copies:
        copy.start()
    for copy in copies:
        copy.wait()


def spread_kernel(piece_cols, own, from_x, from_y, from_xy, after, keep, to_1, to_2, to_3):
    count = from_y.shape[0]
    cap = count // PIECES
    slots = 4 * cap
    group, loc, zb, pair, _ = place()
    source = 2 * group + loc
    m, n = iota((2 * count, count), 0), iota((2 * count, count), 1)
    mq, nq = quotient(m, cap, 2 * count), quotient(n, cap, count)
    m_slot, n_slot = m - cap * mq, n - cap * nq
    m_flip, m_source, m_part = mq >> 3, (mq >> 1) & 3, mq & 1
    wanted = 4 * loc + 2 * (zb ^ m_flip) + m_part
    rows_ok = (m_slot == n_slot) & (nq == wanted)
    total = jnp.zeros((2 * count, piece_cols), F32)
    for k, ref in enumerate((own, from_x, from_y, from_xy)):
        total += dot(hot(rows_ok & (m_source == (source ^ k))), ref[:, :piece_cols])
    m_loc, m_row = (mq >> 2) & 1, m - slots * (mq >> 2)
    n_half, n_row = nq >> 2, n - slots * (nq >> 2)
    hidden_ok = (m_row == n_row) & (n_half == (pair ^ m_flip))
    hidden = dot(hot(hidden_ok & (m_loc == loc)), own[:, piece_cols:]) + dot(
        hot(hidden_ok & (m_loc != loc)), from_x[:, piece_cols:]
    )
    total, hidden = total.astype(BF16), hidden.astype(BF16)
    for ref, flip_zb, flip_pair in ((keep, 0, 0), (to_1, 1, 0), (to_2, 0, 1), (to_3, 1, 1)):
        ref[:, :piece_cols] = total[flip_zb * count : (flip_zb + 1) * count]
        ref[:, piece_cols:] = hidden[flip_pair * count : (flip_pair + 1) * count]


def expert_kernel(
    own, from_x, from_y, from_xy, down, gate, up, ret_own, ret_y, ret_x, stack
):
    count, piece_cols = ret_y.shape
    cap = count // PIECES
    pad = stack.shape[0] // PIECES
    slots = gate.shape[2]
    group, loc, _, _, _ = place()
    source = 2 * group + loc
    m, n = iota((PIECES * pad, count), 0), iota((PIECES * pad, count), 1)
    nq = quotient(n, cap, count)
    n_slot = n - cap * nq
    m_piece, m_slot = m // pad, m % pad
    total = jnp.zeros((PIECES * pad, piece_cols), F32)
    for k, ref in enumerate((own, from_x, from_y, from_xy)):
        match = (m_piece == nq) & (m_slot == (source ^ k) * cap + n_slot)
        total += dot(hot(match), ref[:, :piece_cols])
    slot_rows = total.astype(BF16)
    turned = jnp.zeros((down.shape[1], pad), F32)
    for j in range(PIECES):
        turned += dot_nt(
            down[0, :, j * piece_cols : (j + 1) * piece_cols], slot_rows[j * pad : (j + 1) * pad]
        )
    grad_act = turned.T
    gate_pad = dot(hot(iota((pad, slots), 0) == iota((pad, slots), 1)), gate[0, 0])
    grad_up = (grad_act * gate_pad).astype(BF16)
    for j in range(PIECES):
        part = dot_nt(grad_up, up[0, j * piece_cols : (j + 1) * piece_cols, :])
        stack[j * pad : (j + 1) * pad, :] = part.astype(BF16)
    n, m = iota((4 * count, PIECES * pad), 0), iota((4 * count, PIECES * pad), 1)
    nq = quotient(n, cap, 4 * count)
    n_slot = n - cap * nq
    m_piece, m_slot = m // pad, m % pad
    back_row = jnp.where(nq < 2 * PIECES, (nq >> 3) * 2, ((nq >> 3) - 2) * 2 + 1)
    match = (m_piece == nq % PIECES) & (m_slot == (source ^ back_row) * cap + n_slot)
    back = dot(hot(match), stack[...])
    ret_own[...] = back[:count].astype(BF16)
    ret_y[...] = back[count : 2 * count].astype(BF16)
    ret_x[...] = back[2 * count :].astype(BF16)


def merge_kernel(ret_own, ret_y, from_x, near, far):
    other = from_x[...].astype(F32)
    count = near.shape[0]
    near[...] = (ret_own[...].astype(F32) + other[:count]).astype(BF16)
    far[...] = (ret_y[...].astype(F32) + other[count:]).astype(BF16)


def products(scale, refs, rows_dev, core):
    count = refs[0].shape[0]
    cap = count // PIECES
    slots = 4 * cap
    piece_cols = refs[0].shape[1] - 4 * rows_dev
    rows = jnp.concatenate([ref[:, :piece_cols].astype(F32) for ref in refs], 0).astype(BF16)
    m, n = iota((4 * count, count), 0), iota((4 * count, count), 1)
    mq = quotient(m, cap, 4 * count)
    m_slot = m - cap * mq
    m_part, m_loc, m_source, m_has = mq >> 4, (mq >> 3) & 1, (mq >> 1) & 3, mq & 1
    nq = quotient(n, cap, count)
    n_loc, n_row = nq >> 2, n - slots * (nq >> 2)
    ok = (m_has == m_part) & (m_loc == n_loc) & (m_source * cap + m_slot == n_row)
    place_rows = jnp.where(ok, scale, 0.0).astype(BF16)
    wide = 4 * rows_dev
    every = dot(place_rows, jnp.concatenate([ref[:, piece_cols:] for ref in refs], 1))
    spread = [every[:, k * wide : (k + 1) * wide] for k in range(len(refs))]
    picks = []
    for block in range(4):
        at = block * count
        hidden = jnp.concatenate([value[at : at + count] for value in spread], 0).T
        for k in range(2):
            first = hidden[2 * k * rows_dev : (2 * k + 1) * rows_dev]
            second = hidden[(2 * k + 1) * rows_dev : (2 * k + 2) * rows_dev]
            picks.append(jnp.where(core == 0, first, second).astype(BF16))
    return dot(jnp.concatenate(picks, 0), rows)


def early_kernel(scale, own, from_2, from_3, from_1, swap_own, swap_2, after, total):
    _, _, _, _, core = place()
    refs = (own, from_2, from_3, from_1, swap_own, swap_2)
    total[...] = products(scale, refs, total.shape[0] // 8, core)


def product_kernel(scale, early, swap_3, swap_1, keep, to_xz, to_x, to_z, stage):
    rows_dev = keep.shape[0]
    piece_cols = keep.shape[1] // 2
    _, loc, zb, _, core = place()
    late = products(scale, (swap_3, swap_1), rows_dev, core)
    product = (early[...] + late).astype(BF16)
    for part in range(2):
        cols = slice(part * piece_cols, (part + 1) * piece_cols)
        for k in range(4):
            at = (4 * part + k) * rows_dev
            stage[k, :, cols] = product[at : at + rows_dev]
    for k, out in enumerate((keep, to_z, to_x, to_xz)):
        out[...] = stage[(2 * loc + zb) ^ k]


def tokens_kernel(names, near, far, out):
    count, piece_cols = near.shape
    cap = count // PIECES
    tokens = out.shape[1]
    both = jnp.concatenate([near[...].astype(F32), far[...].astype(F32)], 0).astype(BF16)
    token, lane = iota((tokens, 2 * count), 0), iota((tokens, 2 * count), 1)
    piece = quotient(lane, cap, 2 * count) % PIECES
    match = token == names[:1, : 2 * count]
    for j in range(PIECES):
        total = dot(hot(match & (piece == j)), both).astype(BF16)
        out[0, :, j * piece_cols : (j + 1) * piece_cols] = total


def join_kernel(own, from_xz, from_z, from_x, summed, tokens_hbm, down_hbm, out, sems):
    cols = own.shape[1]
    _, loc, zb, _, _ = place()
    copies = [pltpu.make_async_copy(summed, tokens_hbm, sems.at[4])]
    copies[0].start()
    for k, ref in enumerate((own, from_z, from_x, from_xz)):
        start = pl.multiple_of(((2 * loc + zb) ^ k) * cols, cols)
        out[k] = ref[...].astype(F32)
        copy = pltpu.make_async_copy(out.at[k], down_hbm.at[0, :, pl.ds(start, cols)], sems.at[k])
        copy.start()
        copies.append(copy)
    for copy in copies:
        copy.wait()


VM = pl.BlockSpec(memory_space=pltpu.VMEM)
ANY = pl.BlockSpec(memory_space=pl.ANY)


def call(kernel, outs, args, specs=None, outs_specs=None, scratch=(), flops=0, nbytes=0):
    out_shape = tuple(jax.ShapeDtypeStruct(shape, dtype) for shape, dtype in outs)
    result = pl.pallas_call(
        kernel,
        out_shape=out_shape,
        in_specs=specs or [VM] * len(args),
        out_specs=tuple(outs_specs or [VM] * len(outs)),
        scratch_shapes=list(scratch),
        compiler_params=pltpu.CompilerParams(vmem_limit_bytes=16 * 1024 * 1024),
        cost_estimate=pl.CostEstimate(flops=flops, bytes_accessed=nbytes, transcendentals=0),
    )(*args)
    return result


def hbm(value):
    return pltpu.with_memory_space_constraint(value, pltpu.HBM)


def swap(value, group_flip=0, loc_flip=0, dp_flip=0):
    sizes = [lax.axis_size(axis) for axis in AXES]
    pairs = []
    for g in range(sizes[0]):
        for l in range(sizes[1]):
            for d in range(sizes[2]):
                here = (g * sizes[1] + l) * sizes[2] + d
                there = ((g ^ group_flip) * sizes[1] + (l ^ loc_flip)) * sizes[2] + (d ^ dp_flip)
                pairs.append((here, there))
    return lax.ppermute(value, AXES, pairs)


def local_messages(
    out_grad, slot_token, slot_count, slot_weight, up_weight, down_weight, hidden_saved, gate_saved
):
    model = out_grad.shape[2]
    tokens = out_grad.shape[1]
    cap = slot_token.shape[3]
    hidden_dev = hidden_saved.shape[3]
    replicas = lax.axis_size("dp")
    piece_cols, half, count = model // PIECES, hidden_dev // 2, PIECES * cap
    rows_dev = hidden_dev // replicas
    inputs = (slot_token, slot_count, slot_weight, out_grad, hidden_saved)
    spaces = (pltpu.SMEM, pltpu.SMEM, pltpu.VMEM, pltpu.VMEM, pltpu.VMEM)
    near, far, names = call(
        select_kernel,
        [
            ((count, piece_cols + half), BF16),
            ((count, piece_cols + half), BF16),
            ((8, 128), jnp.int32),
        ],
        [hbm(x) for x in inputs],
        [ANY] * 5,
        scratch=[space(x.shape, x.dtype) for space, x in zip(spaces, inputs)]
        + [pltpu.SemaphoreType.DMA((5,))],
        nbytes=tokens * model * 2,
    )
    from_xy = swap(far, group_flip=1, loc_flip=1)
    from_y = swap(far, group_flip=1)
    from_x = swap(near, loc_flip=1)
    arrived = (near, from_x, from_y, from_xy)
    held = (down_weight, up_weight, gate_saved)
    down, up, gate = call(
        load_kernel,
        [(x.shape, x.dtype) for x in held],
        [hbm(x) for x in held] + [near],
        [ANY] * 4,
        scratch=[pltpu.SemaphoreType.DMA((3,))],
        nbytes=8 * model * hidden_dev,
    )
    message = ((count, piece_cols + half), BF16)
    mine, to_1, to_2, to_3 = call(
        functools.partial(spread_kernel, piece_cols), [message] * 4, arrived + (gate,), [VM] * 4 + [ANY], nbytes=count * model
    )
    from_2 = swap(to_2, dp_flip=4)
    from_3 = swap(to_3, dp_flip=6)
    from_1 = swap(to_1, dp_flip=2)
    pad = -(-4 * cap // 16) * 16
    part = ((count, piece_cols), BF16)
    ret_own, ret_y, ret_x = call(
        expert_kernel,
        [part, part, ((2 * count, piece_cols), BF16)],
        arrived + (down, gate, up),
        scratch=[pltpu.VMEM((PIECES * pad, piece_cols), BF16)],
        flops=4 * pad * model * hidden_dev,
        nbytes=4 * model * hidden_dev,
    )
    back_x = swap(ret_x, loc_flip=1)
    near_sum, far_sum = call(merge_kernel, [part] * 2, (ret_own, ret_y, back_x), nbytes=1 << 18)
    back_y = swap(far_sum, group_flip=1)
    parts = (mine, from_2, from_3, from_1)
    swapped = tuple(swap(x, dp_flip=1) for x in parts)
    block = ((rows_dev, 2 * piece_cols), BF16)
    (early_sum,) = call(
        functools.partial(early_kernel, 1.0 / replicas),
        [((8 * rows_dev, piece_cols), F32)],
        parts + swapped[:2] + (ret_own,),
        [VM] * 6 + [ANY],
        nbytes=1 << 20,
    )
    own, to_xz, to_x, to_z = call(
        functools.partial(product_kernel, 1.0 / replicas),
        [block] * 4,
        (early_sum,) + swapped[2:],
        scratch=[pltpu.VMEM((4, rows_dev, 2 * piece_cols), BF16)],
        nbytes=1 << 20,
    )
    got_xz = swap(to_xz, loc_flip=1, dp_flip=2)
    got_z = swap(to_z, dp_flip=2)
    got_x = swap(to_x, loc_flip=1)
    (summed,) = call(
        tokens_kernel,
        [((1, tokens, model), BF16)],
        (names, near_sum, back_y),
        nbytes=2 << 20,
    )
    input_grad, down_grad = call(
        join_kernel,
        [((1, tokens, model), BF16), ((1, rows_dev, model), F32)],
        (own, got_xz, got_z, got_x, summed),
        outs_specs=[ANY] * 2,
        scratch=[
            pltpu.VMEM((4, rows_dev, 2 * piece_cols), F32),
            pltpu.SemaphoreType.DMA((5,)),
        ],
        nbytes=1 << 20,
    )
    return (input_grad, down_grad)


def local(*args):
    sizes = tuple(lax.axis_size(axis) for axis in AXES)
    model, cap, hidden_dev = args[0].shape[2], args[1].shape[3], args[6].shape[3]
    fits = sizes == (2, 2, 8) and model % (PIECES * 128) == 0
    fits = fits and hidden_dev % 256 == 0 and args[0].shape[1] % 16 == 0 and 4 * cap <= 32
    return (local_messages if fits else local_collectives)(*args)


def solution(mesh):
    return jax.shard_map(
        local,
        mesh=mesh,
        in_specs=(
            P("dp", ("grp", "loc"), None),
            P("dp", ("grp", "loc"), None, None),
            P("dp", ("grp", "loc"), None),
            P("dp", ("grp", "loc"), None, None),
            P("grp", None, "loc"),
            P("grp", "loc", None),
            P("dp", "grp", None, "loc"),
            P("dp", "grp", None, "loc"),
        ),
        out_specs=(P("dp", ("grp", "loc"), None), P("grp", ("loc", "dp"), None)),
        check_vma=False,
    )
```
